128 devices in a mesh: seq: 4 (over x), ep: 32 (over z, y, core).
Axes of the slice: x: 4, y: 4, z: 4, core: 2. Of those that a mesh axis runs over, the one named last changes fastest.
Arguments:
- tokens: bfloat16 [1024, 7168], P(('seq', 'ep')), may hold values from -50 to 50
- out_grad: bfloat16 [1024, 7168], P(('seq', 'ep')), may hold values from -24 to 24
- routes: int32 [1024, 8], P(('seq', 'ep')), may hold values from 0 to 31, all different within a row; in each aligned block of 8 rows (0 to 7, 8 to 15, ...) at most 2 rows name the same one
- gate_fixed: int32 [1024, 8], P(('seq', 'ep')), may hold values from 1 to 65535
- ramp_step: int32 [32], replicated, may hold values from 1 to 8
- norm_gain: float32 [7168], replicated, may hold values from 0.1 to 1.9
- w_gate: bfloat16 [32, 7168, 1024], P('ep', None, 'seq'), may hold values from -0.0625 to 0.0625
- w_up: bfloat16 [32, 7168, 1024], P('ep', None, 'seq'), may hold values from -0.0625 to 0.0625
- w_down: bfloat16 [32, 1024, 7168], P('ep', 'seq'), may hold values from -0.1875 to 0.1875
Outputs:
- mixed: bfloat16 [1024, 7168], P(('seq', 'ep'))
- tokens_grad: bfloat16 [1024, 7168], P(('seq', 'ep'))
- gain_grad: float32 [7168], P(('seq', 'ep'))
- w_gate_grad: bfloat16 [32, 7168, 1024], P('ep', None, 'seq')
- w_up_grad: bfloat16 [32, 7168, 1024], P('ep', None, 'seq')
- w_down_grad: bfloat16 [32, 1024, 7168], P('ep', 'seq')
The draws below stay inside these ranges and needn't reach their ends.
Inputs may be any that keep to these rules, and one draw needn't show every extreme that they name: `routes`: each row names 8 different experts. Within the rows of one device (aligned blocks of 8 rows) no expert is named more than 2 times, and in some such block one expert is named exactly 2 times.
All inputs are finite; a program needn't handle non-finite values.
Results may differ from the reference program's by a relative error of at most 0.023.
Values may be sent and summed in bfloat16 or wider, within the bound.
A program may use at most 128 MiB of HBM per device.

```python
import math
import jax
import jax.numpy as jnp
import numpy as np
from jax import lax

D = 7168
FFW = 1024
TOP = 8
RAMP = 8
TOK_DEV = 8
EXPERTS = 32
CAP = 2
TOKENS = 1024
N_SEQ = 4
N_EP = 32


def draw_tokens(key, part):
    key_base, key_column, key_row = jax.random.split(key, 3)
    column = jnp.exp(jax.random.uniform(key_column, (D,), jnp.float32, 0.0, math.log(10.0)))
    row_scale = jnp.exp(jax.random.uniform(key_row, (TOKENS, 1), jnp.float32, 0.0, math.log(10.0)))
    base = jax.random.normal(key_base, (TOKENS, D), jnp.float32)
    base = jnp.clip(base, -5.0, 5.0)
    return (base * column[None, :] * row_scale / 10.0).astype(jnp.bfloat16)


def draw_ramp_step(key, part):
    key_steps, key_order = jax.random.split(key, 2)
    steps = jax.random.randint(key_steps, (EXPERTS,), 1, RAMP + 1, jnp.int32)
    order = jax.random.permutation(key_order, EXPERTS)
    steps = steps.at[order[0]].set(RAMP)
    steps = steps.at[order[1]].set(1)
    return steps


def plant(drawn, rng, low, top_value):
    extent = drawn.shape
    spot = [jax.random.randint(jax.random.fold_in(rng, axis), (), 0, extent[axis]) for axis in range(len(extent))]
    drawn = drawn.at[tuple(spot)].set(low)
    longest = extent.index(max(extent))
    spot[longest] = (spot[longest] + 1) % extent[longest]
    return drawn.at[tuple(spot)].set(top_value)


def raised(array, own_key, source, target, shards_of, factor):
    owner, partner = [(jnp.arange(array.shape[dim]) // (array.shape[dim] // shards_of)).reshape([-1 if axis == dim else 1 for axis in range(array.ndim)]) for dim in (source, target)]
    chosen = jax.random.permutation(own_key, shards_of)[partner]
    strong = (owner == chosen) | (owner == (partner + shards_of // 2) % shards_of)
    return jnp.where(strong, factor * array, array)


def level_of(own_key, dims, shards, least, top_value):
    level, own = 1.0, jax.random.fold_in(own_key, 6)
    for axis_at, shards_of in shards:
        draws = jnp.exp(jax.random.uniform(jax.random.fold_in(own, axis_at), (shards_of,), jnp.float32, least / len(shards), top_value / len(shards)))
        level = level * jnp.repeat(draws, dims[axis_at] // shards_of).reshape([-1 if axis == axis_at else 1 for axis in range(len(dims))])
    return level


def deal_out(own_key, own, number, rows, amount, top, reach, lean):
    sequence = jax.random.permutation(own_key, amount)
    crowded, common = portions_of(amount, rows * top, reach, lean, True), portions_of(amount, rows * top, reach, lean, False)
    places = jnp.arange(amount)

    def named(sizes, offset_by):
        used = int((sizes > 0).sum())
        fixed = max(1, used // 4)
        shifted = fixed + (places - fixed + offset_by * (used - fixed)) % max(1, amount - fixed)
        return jnp.zeros((amount,), jnp.int32).at[sequence[jnp.where(places < fixed, places, shifted)]].set(jnp.asarray(sizes, jnp.int32))

    sizes = jnp.where(number % 4 == 0, named(crowded, number // 4), named(common, number - number // 4 - 1))
    mixed = jax.random.permutation(jax.random.fold_in(own, 3), amount)
    donor, receiver = mixed[0:amount // 2 * 2:2], mixed[1:amount // 2 * 2:2]
    slack = jnp.minimum(sizes[donor] - 1, reach - sizes[receiver]) // 2
    slack = jnp.where((donor == sequence[0]) | (receiver == sequence[0]) | (sizes[receiver] == 0), 0, jnp.maximum(slack, 0))
    shifted = jax.random.randint(jax.random.fold_in(own, 4), (amount // 2,), 0, 1 << 20) % (slack + 1)
    sizes = sizes.at[donor].add(-shifted).at[receiver].add(shifted)
    items = jnp.searchsorted(jnp.cumsum(sizes), jnp.arange(rows * top), side="right").astype(jnp.int32)
    listing = items.reshape(top, rows).T
    listing = listing[jax.random.permutation(jax.random.fold_in(own, 1), rows)]
    offset_by = jax.random.randint(jax.random.fold_in(own, 2), (rows, 1), 0, top)
    return jnp.take_along_axis(listing, (jnp.arange(top)[None, :] + offset_by) % top, axis=1)


def portions_of(count, total, bound, skew, full):
    loads = [(1 << 20) // math.isqrt(standing ** skew) + 1 for standing in range(1, count + 1)]
    largest = bound if full else min(bound, max(-(-total // count), total * loads[0] // sum(loads)))
    least = 1 if total - largest >= count - 1 else 0
    counts, spare = [largest] + [least] * (count - 1), total - largest - least * (count - 1)
    while spare > 0:
        movable = [i for i in range(1, count) if counts[i] < largest] or [i for i in range(1, count) if counts[i] < bound]
        mass, budget = sum([loads[i] for i in movable]), spare
        for i in movable:
            extra = min(bound - counts[i], max(1, budget * loads[i] // mass), spare)
            counts[i] = counts[i] + extra
            spare = spare - extra
    return np.array(counts)


def noise(stream_key, dims, width, limit, pieces=(), held_as=jnp.bfloat16):
    entries = width * jax.random.normal(stream_key, dims, jnp.float32)
    if pieces:
        entries = entries * level_of(stream_key, dims, pieces, -0.22, 0.18)
    return jnp.clip(entries, -limit, limit).astype(held_as)


def noise_with(own_key, shape, spread, limit, cuts, heavy, held_as=jnp.bfloat16):
    drawn = spread * jax.random.normal(own_key, shape, jnp.float32)
    if cuts:
        drawn = drawn * level_of(own_key, shape, cuts, -0.22, 0.18)
    return jnp.clip(raised(drawn, jax.random.fold_in(own_key, 3), *heavy), -limit, limit).astype(held_as)


def setup_inputs(seed: int = 0) -> dict:
    splits = jax.random.split(jax.random.key(seed), 10)
    tokens = draw_tokens(jax.random.fold_in(splits[9], 71), 0)
    out_grad = noise_with(splits[1], (TOKENS, D), 1.0, 24.0, ((0, 128),), (0, 1, 128, 5.5))
    routes_keys = jax.random.split(jax.random.fold_in(splits[2], 1), TOKENS // TOK_DEV)
    routes_turns = jax.random.permutation(jax.random.fold_in(splits[2], 3), TOKENS // TOK_DEV)
    routes = jax.vmap(lambda own, number: deal_out(jax.random.fold_in(splits[2], 2), own, number, TOK_DEV, EXPERTS, TOP, CAP, 2))(routes_keys, routes_turns).reshape((TOKENS, TOP))
    gate_fixed = plant(jax.random.randint(splits[3], (TOKENS, TOP), 1, 65536), jax.random.fold_in(splits[3], 1), 1, 65535).astype(jnp.int32)
    ramp_step = draw_ramp_step(jax.random.fold_in(splits[9], 71), 0)
    norm_gain = jnp.clip(1.0 + 0.18 * jax.random.normal(splits[5], (D,), jnp.float32), 0.1, 1.9)
    w_gate = noise(splits[6], (EXPERTS, D, FFW), D ** -0.5, 0.0625, ((0, 32), (2, 4)))
    w_up = noise(splits[7], (EXPERTS, D, FFW), D ** -0.5, 0.0625, ((0, 32), (2, 4)))
    w_down = noise(splits[8], (EXPERTS, FFW, D), FFW ** -0.5, 0.1875, ((0, 32), (1, 4)))
    return {"tokens": tokens, "out_grad": out_grad, "routes": routes, "gate_fixed": gate_fixed, "ramp_step": ramp_step, "norm_gain": norm_gain, "w_gate": w_gate, "w_up": w_up, "w_down": w_down}


gate_unit = 65536.0
norm_eps = 1e-06

def reference(tokens, out_grad, routes, gate_fixed, ramp_step, norm_gain, w_gate, w_up, w_down):
    blocks = N_SEQ * N_EP
    per_expert = blocks * CAP
    quarter = FFW // N_SEQ
    tokens_wide = tokens.astype(jnp.float32)
    recip = lax.rsqrt(lax.optimization_barrier(jnp.mean(tokens_wide * tokens_wide, axis=1, keepdims=True)) + norm_eps)
    normed = (tokens_wide * recip * norm_gain[None, :]).astype(jnp.bfloat16)
    flat = routes.reshape(blocks, TOK_DEV * TOP)
    onehot = (flat[:, :, None] == jnp.arange(EXPERTS, dtype=jnp.int32)[None, None, :]).astype(jnp.int32)
    position = lax.optimization_barrier(jnp.sum(jnp.cumsum(onehot, axis=1) * onehot, axis=2)) - 1
    block_ids = jnp.arange(blocks, dtype=jnp.int32)[:, None]
    flat_index = (flat * per_expert + block_ids * CAP + position).reshape(-1).astype(jnp.int32)
    pair_ids = jnp.arange(TOKENS * TOP, dtype=jnp.int32)
    table = jnp.full((EXPERTS * per_expert,), TOKENS * TOP, jnp.int32).at[flat_index].set(pair_ids)
    ramp_pick = ramp_step[routes.reshape(-1)].astype(jnp.float32)
    coef = gate_fixed.reshape(-1).astype(jnp.float32) / gate_unit * ramp_pick / RAMP
    grad_rows = (coef[:, None] * jnp.repeat(out_grad.astype(jnp.float32), TOP, axis=0)).astype(jnp.bfloat16)
    normed_pad = jnp.concatenate([normed, jnp.zeros((1, D), jnp.bfloat16)], axis=0)
    grad_pad = jnp.concatenate([grad_rows, jnp.zeros((1, D), jnp.bfloat16)], axis=0)

    def per_item(item):
        pair_rows, weight_gate, weight_up, weight_down = item
        rows_normed = normed_pad[pair_rows // TOP]
        rows_grad = grad_pad[pair_rows]
        pre_gate = jnp.dot(rows_normed, weight_gate, preferred_element_type=jnp.float32)
        pre_up = jnp.dot(rows_normed, weight_up, preferred_element_type=jnp.float32)
        sigma = jax.nn.sigmoid(pre_gate)
        active = pre_gate * sigma
        hidden = (active * pre_up).astype(jnp.bfloat16)
        hidden_q = hidden.astype(jnp.float32).reshape(per_expert, N_SEQ, quarter)
        down_q = weight_down.astype(jnp.float32).reshape(N_SEQ, quarter, D)
        parts = jnp.einsum('rqf,qfd->qrd', hidden_q, down_q).astype(jnp.bfloat16)
        slot_out = lax.optimization_barrier(jnp.sum(parts.astype(jnp.float32), axis=0)).astype(jnp.bfloat16)
        hidden_grad = jnp.dot(rows_grad, weight_down.T, preferred_element_type=jnp.float32)
        gate_pre_grad = (hidden_grad * pre_up * sigma * (1.0 + pre_gate * (1.0 - sigma))).astype(jnp.bfloat16)
        up_pre_grad = (hidden_grad * active).astype(jnp.bfloat16)
        down_grad = jnp.dot(hidden.T, rows_grad, preferred_element_type=jnp.float32).astype(jnp.bfloat16)
        gate_grad = jnp.dot(rows_normed.T, gate_pre_grad, preferred_element_type=jnp.float32).astype(jnp.bfloat16)
        up_grad = jnp.dot(rows_normed.T, up_pre_grad, preferred_element_type=jnp.float32).astype(jnp.bfloat16)
        gate_q = gate_pre_grad.astype(jnp.float32).reshape(per_expert, N_SEQ, quarter)
        up_q = up_pre_grad.astype(jnp.float32).reshape(per_expert, N_SEQ, quarter)
        wg_q = weight_gate.astype(jnp.float32).reshape(D, N_SEQ, quarter)
        wu_q = weight_up.astype(jnp.float32).reshape(D, N_SEQ, quarter)
        back_parts = (jnp.einsum('rqf,dqf->qrd', gate_q, wg_q) + jnp.einsum('rqf,dqf->qrd', up_q, wu_q)).astype(jnp.bfloat16)
        slot_back = lax.optimization_barrier(jnp.sum(back_parts.astype(jnp.float32), axis=0)).astype(jnp.bfloat16)
        return (slot_out, slot_back, gate_grad, up_grad, down_grad)
    slot_out, slot_back, w_gate_grad, w_up_grad, w_down_grad = lax.map(per_item, (table.reshape(EXPERTS, per_expert), w_gate, w_up, w_down))
    picked_out = slot_out.reshape(-1, D)[flat_index].astype(jnp.float32).reshape(TOKENS, TOP, D)
    picked_back = slot_back.reshape(-1, D)[flat_index].astype(jnp.float32).reshape(TOKENS, TOP, D)
    mixed = lax.optimization_barrier(jnp.sum(coef.reshape(TOKENS, TOP, 1) * picked_out, axis=1)).astype(jnp.bfloat16)
    normed_grad = lax.optimization_barrier(jnp.sum(picked_back, axis=1))
    gain_grad = lax.optimization_barrier(jnp.sum(normed_grad * tokens_wide * recip, axis=0))
    scaled = norm_gain[None, :] * normed_grad
    inner = lax.optimization_barrier(jnp.sum(scaled * tokens_wide, axis=1, keepdims=True))
    tokens_grad = (recip * scaled - tokens_wide * recip * recip * recip * inner / D).astype(jnp.bfloat16)
    return (mixed, tokens_grad, gain_grad, w_gate_grad, w_up_grad, w_down_grad)
```

```python
import functools

import jax
import jax.numpy as jnp
from jax import lax
from jax.experimental import pallas as pl
from jax.experimental.pallas import tpu as pltpu
from jax.sharding import PartitionSpec as P

MESH = pl.DeviceIdType.MESH
RAMP = 8.0
GATE_UNIT = 65536.0
NORM_EPS = 1e-06

TOK = 8
TOP = 8
PAIRS = TOK * TOP
D = 7168
HID = 256
NX, NE = 4, 32
SEG = 4
WIDE = D // SEG
WA = 1152
WB = WIDE - WA
MSG = 512
BF = jnp.bfloat16
F32 = jnp.float32


def dot(a, b):
    return lax.dot_general(a, b, (((1,), (0,)), ((), ())), preferred_element_type=F32)


def dot_nt(a, b):
    return lax.dot_general(a, b, (((1,), (1,)), ((), ())), preferred_element_type=F32)


def dot_tn(a, b):
    return lax.dot_general(a, b, (((0,), (0,)), ((), ())), preferred_element_type=F32)


def iota(shape, dim):
    return lax.broadcasted_iota(jnp.int32, shape, dim)


def pair_table(routes_ref, gate_ref, ramp_ref, z, y, c):
    rep = (iota((PAIRS, TOK), 0) // TOP == iota((PAIRS, TOK), 1)).astype(F32)
    pick = iota((PAIRS, TOP), 0) % TOP == iota((PAIRS, TOP), 1)
    pick_t = iota((TOP, PAIRS), 1) % TOP == iota((TOP, PAIRS), 0)

    def column(v):
        return jnp.sum(jnp.where(pick, dot(rep, v), 0.0), axis=1, keepdims=True)

    routes = routes_ref[...].astype(F32)
    gate = gate_ref[...]
    route_col = column(routes)
    route_row = jnp.sum(
        jnp.where(pick_t, lax.dot_general(routes, rep, (((0,), (1,)), ((), ())), preferred_element_type=F32), 0.0),
        axis=0, keepdims=True)
    gate_col = column((gate >> 8).astype(F32)) * 256.0 + column((gate & 255).astype(F32))
    same = route_col.astype(jnp.int32) == iota((PAIRS, NE), 1)
    ramp_col = jnp.sum(jnp.where(same, ramp_ref[...].astype(F32), 0.0), axis=1, keepdims=True)
    coef = gate_col / GATE_UNIT * ramp_col / RAMP
    high = coef.astype(BF).astype(F32)
    low = coef - high

    before = (route_col == route_row) & (iota((PAIRS, PAIRS), 0) < iota((PAIRS, PAIRS), 1))
    row = jnp.sum(before.astype(F32), axis=0, keepdims=True).astype(jnp.int32)
    e = route_row.astype(jnp.int32)
    rel = (((e >> 3) - z) & 3) * 8 + ((((e >> 1) & 3) - y) & 3) * 2 + (((e & 1) - c) & 1)
    slot = (rel * 5) & 31
    place = (iota((PAIRS, PAIRS), 0) == slot * 2 + row).astype(BF)

    lane = iota((PAIRS, 128), 1)
    first, grad = lane < 64, ((lane >> 3) & 1) == 1
    mine = (iota((PAIRS, 128), 0) // TOP) == (lane & 7)
    value = jnp.where(first, jnp.where(grad, high, 1.0), jnp.where(grad, low, 0.0))
    return dot(place, jnp.where(mine, value, 0.0).astype(BF)).astype(BF)


def spread_table(pairs):
    m = iota((MSG, PAIRS), 0)
    expand = ((m >> 4) * 2 + (m & 1) == iota((MSG, PAIRS), 1)).astype(BF)
    m, lane = iota((MSG, 128), 0), iota((MSG, 128), 1)
    keep = (((m >> 2) & 3) == ((lane >> 4) & 3)) & (((m >> 1) & 1) == ((lane >> 3) & 1))
    return jnp.where(keep, dot(expand, pairs), 0.0).astype(BF)


def shuffles():
    def table(o, m):
        return (((o >> 1) & 15) * 16 + ((o >> 5) & 3) * 4 + (o >> 7) * 2 + (o & 1) == m).astype(BF)

    shape = (256, 256)
    return table(iota(shape, 0), iota(shape, 1)), table(iota(shape, 1), iota(shape, 0))


def layer(
    tok_ref, og_ref, routes_ref, gate_ref, ramp_ref, gain_ref, wg_hbm, wu_hbm, wd_hbm,
    mixed_ref, tg_ref, gq_ref, x_hbm, g_hbm, h_ref, gp_ref, up_ref,
    wg, wu, wd, tab, tbm, spread, perm, perm_t, sa, ra, sb, rb, xs, gs, acc, st_a, st_b,
    qa, qb, half1, half3, l1, l3, ca, cb, ys, xb, ng, mx, gsend, gx, gpart, gl,
    w_sem, out_sem, tb_s, tb_r, sa_s, sa_r, fw_s, fw_r, f2_s, f2_r, sb_s, sb_r,
    hf_s, hf_r, l_s, l_r, qb_s, qb_r, ca_s, ca_r, ys_s, ys_r, gx_s, gx_r, gl_s, gl_r,
):
    sx = lax.axis_index("seq")
    me = lax.axis_index("ep")
    z, y, c = me // 8, lax.rem(me // 2, 4), lax.rem(me, 2)

    def along(step):
        return {"seq": lax.rem(sx + step, 4)}

    def peer(i, back):
        b = lax.rem(i * 13, 32)
        dz, dy, dc = b // 8, lax.rem(b // 2, 4), lax.rem(b, 2)
        if back:
            dz, dy = 4 - dz, 4 - dy
        return {"ep": lax.rem(z + dz, 4) * 8 + lax.rem(y + dy, 4) * 2 + lax.rem(c + dc, 2)}

    def remote(src, dst, send, recv, to):
        return pltpu.make_async_remote_copy(src, dst, send, recv, device_id=to, device_id_type=MESH)

    barrier = pltpu.get_barrier_semaphore()
    for step in (1, 2, 3):
        pl.semaphore_signal(barrier, inc=1, device_id=along(step), device_id_type=MESH)

    def greet(i, _):
        pl.semaphore_signal(barrier, inc=1, device_id=peer(i, False), device_id_type=MESH)
        return 0

    lax.fori_loop(1, NE, greet, 0)

    loads = [pltpu.make_async_copy(a, b, w_sem.at[i]) for i, (a, b) in enumerate(((wg_hbm, wg), (wu_hbm, wu), (wd_hbm, wd)))]
    for load in loads:
        load.start()

    tokens = tok_ref[...].astype(F32)
    recip = lax.rsqrt(jnp.sum(tokens * tokens, axis=1, keepdims=True) / D + NORM_EPS)
    for s in range(SEG):
        cols = slice(s * WIDE, (s + 1) * WIDE)
        normed = tok_ref[:, cols].astype(F32) * recip * gain_ref[:, cols]
        both = jnp.concatenate([normed, og_ref[:, cols].astype(F32)], axis=0).astype(BF)
        tab[16 * s:16 * s + 16, :] = both
        tab[64 + 16 * s:80 + 16 * s, :] = both
    pairs = pair_table(routes_ref, gate_ref, ramp_ref, z, y, c)
    tbm[0, :, 0:WB] = tab[0:64, WA:WIDE]
    tbm[0, :, WB:WB + 128] = pairs
    pl.semaphore_wait(barrier, 34)

    tb_copies = [remote(tbm.at[0], tbm.at[step], tb_s.at[step - 1], tb_r.at[step - 1], along(step)) for step in (1, 2, 3)]
    for copy in tb_copies:
        copy.start()

    spread[0] = spread_table(pairs)
    for chunk in range(4):
        rows = slice(128 * chunk, 128 * chunk + 128)
        sa[rows, :] = dot(spread[0, rows, :], tab[:, 0:WA]).astype(BF)

        def send_a(i, _, chunk=chunk):
            at = pl.ds(pl.multiple_of(16 * i, 16), 16)
            remote(sa.at[at, :], ra.at[0, at, :], sa_s, sa_r.at[chunk], peer(i, False)).start()
            return 0

        lax.fori_loop(max(8 * chunk, 1), 8 * chunk + 8, send_a, 0)
    ra[0, 0:16, :] = sa[0:16, :]
    p, p_t = shuffles()
    perm[...] = p
    perm_t[...] = p_t

    for k in range(4):
        if k:
            tb_copies[k - 1].wait_recv()
            spread[k] = spread_table(tbm[k, :, WB:WB + 128])
        twice = jnp.concatenate([tbm[k, :, 0:WB]] * 2, axis=0)
        for chunk in range(4):
            rows = slice(128 * chunk, 128 * chunk + 128)
            sb[8 * chunk:8 * chunk + 8, 16 * k:16 * k + 16, :] = (
                dot(spread[k, rows, :], twice).astype(BF).reshape(8, 16, WB))

    def send_b(i, _):
        remote(sb.at[i], rb.at[i], sb_s, sb_r, peer(i, False)).start()
        return 0

    lax.fori_loop(1, NE, send_b, 0)
    rb[0] = sb[0]

    forward = []
    for chunk in range(4):
        rows = pl.ds(128 * chunk, 128)
        skip = 16 if chunk == 0 else 0
        got = pl.ds(128 * chunk + skip, 128 - skip)
        remote(sa.at[got, :], ra.at[0, got, :], sa_s, sa_r.at[chunk], along(1)).wait_recv()
        for way, (step, land) in enumerate(((1, 1), (3, 3))):
            k = 2 * chunk + way
            copy = remote(ra.at[0, rows, :], ra.at[land, rows, :], fw_s.at[k], fw_r.at[k], along(step))
            copy.start()
            forward.append(copy)

    def into_rows(value, row, col, width):
        out = dot(perm[...], value).astype(BF)
        for arr, ref in ((0, xs), (1, gs)):
            for s in range(SEG):
                at = (4 * arr + s) * 32
                ref[row:row + 32, s * WIDE + col:s * WIDE + col + width] = out[at:at + 32]

    def multiply(row, count, col, width):
        rows = slice(row, row + count)

        def one(s, _):
            cols = pl.ds(pl.multiple_of(s * WIDE + col, 128), width)
            left = xs[rows, cols]
            acc[0, rows, :] += dot(left, wg[cols, :])
            acc[1, rows, :] += dot(left, wu[cols, :])
            acc[2, rows, :] += dot_nt(gs[rows, cols], wd[:, cols])
            return 0

        lax.fori_loop(0, SEG, one, 0)

    acc[...] = jnp.zeros_like(acc)
    for load in loads:
        load.wait()

    def arrived(k):
        for g in range(2):
            into_rows(ra[k, 256 * g:256 * g + 256, :], 64 * k + 32 * g, 0, WA)
        multiply(64 * k, 64, 0, WA)

    arrived(0)
    further = []
    for chunk in range(4):
        for way in range(2):
            forward[2 * chunk + way].wait_recv()
        rows = pl.ds(128 * chunk, 128)
        land, step = (1, 1) if chunk < 2 else (3, 3)
        copy = remote(ra.at[land, rows, :], ra.at[2, rows, :], f2_s.at[chunk], f2_r.at[chunk], along(step))
        copy.start()
        further.append(copy)
    arrived(1)
    arrived(3)
    remote(sb.at[pl.ds(1, 31)], rb.at[pl.ds(1, 31)], sb_s, sb_r, along(1)).wait_recv()
    for k in range(4):
        for g in range(2):
            into_rows(rb[16 * g:16 * g + 16, 16 * k:16 * k + 16, :].reshape(256, WB), 64 * k + 32 * g, WA, WB)
    multiply(0, 256, WA, WB)
    for copy in further:
        copy.wait_recv()
    arrived(2)
    keep = [pltpu.make_async_copy(xs, x_hbm, out_sem.at[0]), pltpu.make_async_copy(gs, g_hbm, out_sem.at[1])]
    for copy in keep:
        copy.start()

    gate, up, back = acc[0], acc[1], acc[2]
    sig = jax.nn.sigmoid(gate)
    act = gate * sig
    h_ref[...] = (act * up).astype(BF)
    gp_ref[...] = (back * up * sig * (1.0 + gate * (1.0 - sig))).astype(BF)
    up_ref[...] = (back * act).astype(BF)

    def parts(k, col, width, st):
        rows = slice(64 * k, 64 * k + 64)

        def one(s, _):
            cols = pl.ds(pl.multiple_of(s * WIDE + col, 128), width)
            near = (dot_nt(gp_ref[rows, :], wg[cols, :]) + dot_nt(up_ref[rows, :], wu[cols, :])).astype(BF)
            far = dot(h_ref[rows, :], wd[:, cols]).astype(BF)
            for g in range(2):
                st[g, pl.ds(pl.multiple_of(32 * s, 32), 32), :] = near[32 * g:32 * g + 32]
                st[g, pl.ds(pl.multiple_of(128 + 32 * s, 32), 32), :] = far[32 * g:32 * g + 32]
            return 0

        lax.fori_loop(0, SEG, one, 0)

    def parts_a(k):
        parts(k, 0, WA, st_a)
        for g in range(2):
            qa[k, 256 * g:256 * g + 256, :] = dot(perm_t[...], st_a[g]).astype(BF)

    parts_a(2)
    low, high = pl.ds(0, 256), pl.ds(256, 256)
    halves = [
        remote(qa.at[2, low, :], half1, hf_s.at[0], hf_r.at[0], along(3)),
        remote(qa.at[2, high, :], half3, hf_s.at[1], hf_r.at[1], along(1)),
    ]
    for copy in halves:
        copy.start()
    for k in range(4):
        parts(k, WA, WB, st_b)
        for g in range(2):
            qb[16 * g:16 * g + 16, 16 * k:16 * k + 16, :] = dot(perm_t[...], st_b[g]).astype(BF).reshape(16, 16, WB)

    def return_b(i, _):
        remote(qb.at[i], cb.at[i], qb_s, qb_r, peer(i, True)).start()
        return 0

    lax.fori_loop(1, NE, return_b, 0)
    cb[0] = qb[0]

    sums = {}

    def send_sum(k, chunk):
        rows = pl.ds(128 * chunk, 128)
        land, step, way = (l1, 3, 0) if k == 1 else (l3, 1, 1)
        sem = 2 * chunk + way
        copy = remote(qa.at[k, rows, :], land.at[rows, :], l_s.at[sem], l_r.at[sem], along(step))
        copy.start()
        sums[k, chunk] = copy

    def add_half(k, chunk):
        rows = slice(128 * chunk, 128 * chunk + 128)
        other = half1[rows, :] if k == 1 else half3[128 * chunk - 256:128 * chunk - 128, :]
        qa[k, rows, :] = (qa[k, rows, :].astype(F32) + other.astype(F32)).astype(BF)

    parts_a(1)
    send_sum(1, 2)
    parts_a(3)
    send_sum(3, 0)
    halves[0].wait_recv()
    halves[1].wait_recv()
    add_half(1, 0)
    send_sum(1, 0)
    add_half(3, 2)
    send_sum(3, 2)
    send_sum(1, 3)
    send_sum(3, 1)
    add_half(1, 1)
    send_sum(1, 1)
    add_half(3, 3)
    send_sum(3, 3)
    parts_a(0)
    for chunk in (0, 2, 1, 3):
        rows = slice(128 * chunk, 128 * chunk + 128)
        sums[1, chunk].wait_recv()
        sums[3, chunk].wait_recv()
        total = qa[0, rows, :].astype(F32) + l1[rows, :].astype(F32) + l3[rows, :].astype(F32)
        qa[0, rows, :] = total.astype(BF)

        def return_a(i, _):
            at = pl.ds(pl.multiple_of(16 * i, 16), 16)
            remote(qa.at[0, at, :], ca.at[at, :], ca_s, ca_r, peer(i, True)).start()
            return 0

        lax.fori_loop(max(8 * chunk, 1), 8 * chunk + 8, return_a, 0)
    ca[0:16, :] = qa[0, 0:16, :]

    def fold(k, value):
        out = dot_tn(spread[k], value)
        return out[0:64] + out[64:128]

    remote(qb.at[pl.ds(1, 31)], cb.at[pl.ds(1, 31)], qb_s, qb_r, along(1)).wait_recv()
    ys_copies = []
    for k in (2, 1, 3):
        ys[k] = fold(k, cb[:, 16 * k:16 * k + 16, :].reshape(MSG, WB)).astype(BF)
        copy = remote(ys.at[k], xb.at[k], ys_s.at[k - 1], ys_r.at[k - 1], along(4 - k))
        copy.start()
        ys_copies.append(copy)
    mine_b = fold(0, cb[:, 0:16, :].reshape(MSG, WB))
    for copy in ys_copies:
        copy.wait_recv()
    for k in (1, 2, 3):
        mine_b = mine_b + xb[k].astype(F32)
    for s in range(SEG):
        cols = slice(s * WIDE + WA, (s + 1) * WIDE)
        ng[:, cols] = mine_b[16 * s:16 * s + 8]
        mx[:, cols] = mine_b[16 * s + 8:16 * s + 16]
    back_rows = pl.ds(16, MSG - 16)
    remote(qa.at[0, back_rows, :], ca.at[back_rows, :], ca_s, ca_r, along(1)).wait_recv()
    mine_a = fold(0, ca[...])
    for s in range(SEG):
        cols = slice(s * WIDE, s * WIDE + WA)
        ng[:, cols] = mine_a[16 * s:16 * s + 8]
        mx[:, cols] = mine_a[16 * s + 8:16 * s + 16]

    tokens = tok_ref[...].astype(F32)
    grad = ng[...]
    term = jnp.sum(grad * tokens * recip, axis=0, keepdims=True)
    gsend[...] = jnp.zeros_like(gsend)
    for j in range(D // 128):
        at = (j // 14) * 16 + j % 14
        gsend[at:at + 1, :] = term[:, 128 * j:128 * j + 128]

    def quarter(step):
        return gsend.at[pl.ds(pl.multiple_of(lax.rem(sx + step, 4) * 16, 16), 16), :]

    gx_copies = [remote(quarter(step), gx.at[step - 1], gx_s.at[step - 1], gx_r.at[step - 1], along(step)) for step in (1, 2, 3)]
    for copy in gx_copies:
        copy.start()
    mixed_ref[...] = mx[...].astype(BF)
    for copy in gx_copies:
        copy.wait_recv()
    gpart[...] = gsend[pl.ds(pl.multiple_of(sx * 16, 16), 16), :] + gx[0] + gx[1] + gx[2]

    def send_gain(i, _):
        remote(gpart, gl.at[i], gl_s, gl_r, peer(i, False)).start()
        return 0

    lax.fori_loop(1, NE, send_gain, 0)
    gl[0] = gpart[...]
    scaled = gain_ref[...] * grad
    inner = jnp.sum(scaled * tokens, axis=1, keepdims=True)
    tg_ref[...] = (recip * scaled - tokens * (recip * recip * recip * inner / D)).astype(BF)
    remote(gl.at[pl.ds(1, 31)], gl.at[pl.ds(1, 31)], gl_s, gl_r, along(1)).wait_recv()
    gq_ref[...] = jnp.sum(gl[...], axis=0)

    for copy in tb_copies + forward + further + halves + list(sums.values()) + ys_copies + gx_copies:
        copy.wait_send()
    remote(sa.at[back_rows, :], sa.at[back_rows, :], sa_s, sa_r.at[0], along(1)).wait_send()
    remote(sb.at[pl.ds(1, 31)], rb.at[pl.ds(1, 31)], sb_s, sb_r, along(1)).wait_send()
    remote(qb.at[pl.ds(1, 31)], cb.at[pl.ds(1, 31)], qb_s, qb_r, along(1)).wait_send()
    remote(qa.at[0, back_rows, :], ca.at[back_rows, :], ca_s, ca_r, along(1)).wait_send()
    remote(gl.at[pl.ds(1, 31)], gl.at[pl.ds(1, 31)], gl_s, gl_r, along(1)).wait_send()
    for copy in keep:
        copy.wait()


def on_device(tokens, out_grad, routes, gate_fixed, ramp_step, norm_gain, w_gate, w_up, w_down):
    vmem = pl.BlockSpec(memory_space=pltpu.VMEM)
    hbm = pl.BlockSpec(memory_space=pl.ANY)
    dma = pltpu.SemaphoreType.DMA
    outs = pl.pallas_call(
        layer,
        name="layer",
        out_shape=(
            jax.ShapeDtypeStruct((TOK, D), BF),
            jax.ShapeDtypeStruct((TOK, D), BF),
            jax.ShapeDtypeStruct((16, 128), F32),
            jax.ShapeDtypeStruct((256, D), BF),
            jax.ShapeDtypeStruct((256, D), BF),
            jax.ShapeDtypeStruct((256, HID), BF),
            jax.ShapeDtypeStruct((256, HID), BF),
            jax.ShapeDtypeStruct((256, HID), BF),
        ),
        in_specs=[vmem] * 6 + [hbm] * 3,
        out_specs=(vmem, vmem, vmem, hbm, hbm, vmem, vmem, vmem),
        scratch_shapes=[
            pltpu.VMEM((D, HID), BF), pltpu.VMEM((D, HID), BF), pltpu.VMEM((HID, D), BF),
            pltpu.VMEM((128, WIDE), BF),
            pltpu.VMEM((4, 64, WB + 128), BF),
            pltpu.VMEM((4, MSG, 128), BF),
            pltpu.VMEM((256, 256), BF), pltpu.VMEM((256, 256), BF),
            pltpu.VMEM((MSG, WA), BF), pltpu.VMEM((4, MSG, WA), BF),
            pltpu.VMEM((NE, 64, WB), BF), pltpu.VMEM((NE, 64, WB), BF),
            pltpu.VMEM((256, D), BF), pltpu.VMEM((256, D), BF),
            pltpu.VMEM((3, 256, HID), F32),
            pltpu.VMEM((2, 256, WA), BF), pltpu.VMEM((2, 256, WB), BF),
            pltpu.VMEM((4, MSG, WA), BF), pltpu.VMEM((NE, 64, WB), BF),
            pltpu.VMEM((256, WA), BF), pltpu.VMEM((256, WA), BF),
            pltpu.VMEM((MSG, WA), BF), pltpu.VMEM((MSG, WA), BF),
            pltpu.VMEM((MSG, WA), BF), pltpu.VMEM((NE, 64, WB), BF),
            pltpu.VMEM((4, 64, WB), BF), pltpu.VMEM((4, 64, WB), BF),
            pltpu.VMEM((TOK, D), F32), pltpu.VMEM((TOK, D), F32),
            pltpu.VMEM((64, 128), F32), pltpu.VMEM((3, 16, 128), F32),
            pltpu.VMEM((16, 128), F32), pltpu.VMEM((NE, 16, 128), F32),
            dma((3,)), dma((2,)), dma((3,)), dma((3,)), dma, dma((4,)), dma((8,)), dma((8,)), dma((4,)), dma((4,)), dma, dma,
            dma((2,)), dma((2,)), dma((8,)), dma((8,)), dma, dma, dma, dma, dma((3,)), dma((3,)), dma((3,)), dma((3,)), dma, dma,
        ],
        compiler_params=pltpu.CompilerParams(collective_id=0, has_side_effects=True, vmem_limit_bytes=60 * 2**20),
        cost_estimate=pl.CostEstimate(flops=8 * 10**9, bytes_accessed=20 * 10**6, transcendentals=65536),
    )(tokens, out_grad, routes, gate_fixed, ramp_step.reshape(1, NE), norm_gain.reshape(1, D), w_gate[0], w_up[0], w_down[0])
    mixed, tokens_grad, quarter, rows_x, rows_g, hidden, gate_pre, up_pre = outs
    gain_grad = lax.dynamic_slice(quarter.reshape(-1), (lax.axis_index("ep") * 56,), (56,))
    w_gate_grad = dot_tn(rows_x, gate_pre).astype(BF)[None]
    w_up_grad = dot_tn(rows_x, up_pre).astype(BF)[None]
    w_down_grad = dot_tn(hidden, rows_g).astype(BF)[None]
    return (mixed, tokens_grad, gain_grad, w_gate_grad, w_up_grad, w_down_grad)


def solution(mesh):
    return jax.shard_map(
        on_device,
        mesh=mesh,
        in_specs=(
            P(("seq", "ep"), None),
            P(("seq", "ep"), None),
            P(("seq", "ep"), None),
            P(("seq", "ep"), None),
            P(),
            P(),
            P("ep", None, "seq"),
            P("ep", None, "seq"),
            P("ep", "seq", None),
        ),
        out_specs=(
            P(("seq", "ep"), None),
            P(("seq", "ep"), None),
            P(("seq", "ep")),
            P("ep", None, "seq"),
            P("ep", None, "seq"),
            P("ep", "seq", None),
        ),
        check_vma=False,
    )
```

```python
import functools

import jax
import jax.numpy as jnp
from jax import lax
from jax.experimental import pallas as pl
from jax.experimental.pallas import tpu as pltpu
from jax.sharding import PartitionSpec as P

MESH = pl.DeviceIdType.MESH
RAMP = 8.0
GATE_UNIT = 65536.0
NORM_EPS = 1e-06

TOK = 8
TOP = 8
PAIRS = TOK * TOP
D = 7168
HID = 256
NX, NE = 4, 32
SEG = 4
WIDE = D // SEG
WA = 1152
WB = WIDE - WA
MSG = 512
PLACE = {0: 0, 1: 1, 3: 2, 2: 3}
BF = jnp.bfloat16
F32 = jnp.float32


def dot(a, b):
    return lax.dot_general(a, b, (((1,), (0,)), ((), ())), preferred_element_type=F32)


def dot_nt(a, b):
    return lax.dot_general(a, b, (((1,), (1,)), ((), ())), preferred_element_type=F32)


def dot_tn(a, b):
    return lax.dot_general(a, b, (((0,), (0,)), ((), ())), preferred_element_type=F32)


def iota(shape, dim):
    return lax.broadcasted_iota(jnp.int32, shape, dim)


def pair_table(routes_ref, gate_ref, ramp_ref, z, y, c):
    rep = (iota((PAIRS, TOK), 0) // TOP == iota((PAIRS, TOK), 1)).astype(F32)
    pick = iota((PAIRS, TOP), 0) % TOP == iota((PAIRS, TOP), 1)
    pick_t = iota((TOP, PAIRS), 1) % TOP == iota((TOP, PAIRS), 0)

    def column(v):
        return jnp.sum(jnp.where(pick, dot(rep, v), 0.0), axis=1, keepdims=True)

    routes = routes_ref[...].astype(F32)
    gate = gate_ref[...]
    route_col = column(routes)
    route_row = jnp.sum(
        jnp.where(pick_t, lax.dot_general(routes, rep, (((0,), (1,)), ((), ())), preferred_element_type=F32), 0.0),
        axis=0, keepdims=True)
    gate_col = column((gate >> 8).astype(F32)) * 256.0 + column((gate & 255).astype(F32))
    same = route_col.astype(jnp.int32) == iota((PAIRS, NE), 1)
    ramp_col = jnp.sum(jnp.where(same, ramp_ref[...].astype(F32), 0.0), axis=1, keepdims=True)
    coef = gate_col / GATE_UNIT * ramp_col / RAMP
    high = coef.astype(BF).astype(F32)
    low = coef - high

    before = (route_col == route_row) & (iota((PAIRS, PAIRS), 0) < iota((PAIRS, PAIRS), 1))
    row = jnp.sum(before.astype(F32), axis=0, keepdims=True).astype(jnp.int32)
    e = route_row.astype(jnp.int32)
    rel = (((e >> 3) - z) & 3) * 8 + ((((e >> 1) & 3) - y) & 3) * 2 + (((e & 1) - c) & 1)
    slot = (rel * 5) & 31
    place = (iota((PAIRS, PAIRS), 0) == slot * 2 + row).astype(BF)

    lane = iota((PAIRS, 128), 1)
    first, grad = lane < 64, ((lane >> 3) & 1) == 1
    mine = (iota((PAIRS, 128), 0) // TOP) == (lane & 7)
    value = jnp.where(first, jnp.where(grad, high, 1.0), jnp.where(grad, low, 0.0))
    return dot(place, jnp.where(mine, value, 0.0).astype(BF)).astype(BF)


def spread_table(pairs):
    m = iota((MSG, PAIRS), 0)
    expand = ((m >> 4) * 2 + (m & 1) == iota((MSG, PAIRS), 1)).astype(BF)
    m, lane = iota((MSG, 128), 0), iota((MSG, 128), 1)
    keep = (((m >> 2) & 3) == ((lane >> 4) & 3)) & (((m >> 1) & 1) == ((lane >> 3) & 1))
    return jnp.where(keep, dot(expand, pairs), 0.0).astype(BF)


def shuffles():
    def table(o, m):
        return (((o >> 1) & 15) * 16 + ((o >> 5) & 3) * 4 + (o >> 7) * 2 + (o & 1) == m).astype(BF)

    shape = (256, 256)
    return table(iota(shape, 0), iota(shape, 1)), table(iota(shape, 1), iota(shape, 0))


def layer(
    tok_ref, og_ref, routes_ref, gate_ref, ramp_ref, gain_ref, wg_hbm, wu_hbm, wd_hbm,
    mixed_ref, tg_ref, gq_ref, x_hbm, g_hbm, h_ref, gp_ref, up_ref,
    wg, wu, wd, tab, tbm, spread, perm, perm_t, sa, ra, sb, rb, xs, gs, acc, st_a, st_b,
    qa, qb, half1, half3, l1, l3, ca, cb, ys, xb, ng, mx, gacc, gsend, gx, gpart, gl,
    w_sem, out_sem, tb_s, tb_r, sa_s, sa_r, fw_s, fw_r, f2_s, f2_r, sb_s, sb_r,
    hf_s, hf_r, l_s, l_r, qb_s, qb_r, ca_s, ca_r, ys_s, ys_r, gx_s, gx_r, gl_s, gl_r,
):
    sx = lax.axis_index("seq")
    me = lax.axis_index("ep")
    z, y, c = me // 8, lax.rem(me // 2, 4), lax.rem(me, 2)

    def along(step):
        return {"seq": lax.rem(sx + step, 4)}

    def peer(i, back):
        b = lax.rem(i * 13, 32)
        dz, dy, dc = b // 8, lax.rem(b // 2, 4), lax.rem(b, 2)
        if back:
            dz, dy = 4 - dz, 4 - dy
        return {"ep": lax.rem(z + dz, 4) * 8 + lax.rem(y + dy, 4) * 2 + lax.rem(c + dc, 2)}

    def remote(src, dst, send, recv, to):
        return pltpu.make_async_remote_copy(src, dst, send, recv, device_id=to, device_id_type=MESH)

    barrier = pltpu.get_barrier_semaphore()
    for step in (1, 2, 3):
        pl.semaphore_signal(barrier, inc=1, device_id=along(step), device_id_type=MESH)

    def greet(i, _):
        pl.semaphore_signal(barrier, inc=1, device_id=peer(i, False), device_id_type=MESH)
        return 0

    lax.fori_loop(1, NE, greet, 0)

    loads = [pltpu.make_async_copy(a, b, w_sem.at[i]) for i, (a, b) in enumerate(((wg_hbm, wg), (wu_hbm, wu), (wd_hbm, wd)))]
    for load in loads:
        load.start()

    tokens = tok_ref[...].astype(F32)
    recip = lax.rsqrt(jnp.sum(tokens * tokens, axis=1, keepdims=True) / D + NORM_EPS)
    for s in range(SEG):
        cols = slice(s * WIDE, (s + 1) * WIDE)
        normed = tok_ref[:, cols].astype(F32) * recip * gain_ref[:, cols]
        both = jnp.concatenate([normed, og_ref[:, cols].astype(F32)], axis=0).astype(BF)
        tab[16 * s:16 * s + 16, :] = both
        tab[64 + 16 * s:80 + 16 * s, :] = both
    pairs = pair_table(routes_ref, gate_ref, ramp_ref, z, y, c)
    tbm[0, :, 0:WB] = tab[0:64, WA:WIDE]
    tbm[0, :, WB:WB + 128] = pairs
    pl.semaphore_wait(barrier, 34)

    tb_copies = [remote(tbm.at[0], tbm.at[step], tb_s.at[step - 1], tb_r.at[step - 1], along(step)) for step in (1, 2, 3)]
    for copy in tb_copies:
        copy.start()

    spread[0] = spread_table(pairs)
    for chunk in range(4):
        rows = slice(128 * chunk, 128 * chunk + 128)
        sa[rows, :] = dot(spread[0, rows, :], tab[:, 0:WA]).astype(BF)

        def send_a(i, _, chunk=chunk):
            at = pl.ds(pl.multiple_of(16 * i, 16), 16)
            remote(sa.at[at, :], ra.at[0, at, :], sa_s, sa_r.at[chunk], peer(i, False)).start()
            return 0

        lax.fori_loop(max(8 * chunk, 1), 8 * chunk + 8, send_a, 0)
    ra[0, 0:16, :] = sa[0:16, :]
    p, p_t = shuffles()
    perm[...] = p
    perm_t[...] = p_t

    forward = []

    def send_forward(chunk):
        rows = pl.ds(128 * chunk, 128)
        skip = 16 if chunk == 0 else 0
        got = pl.ds(128 * chunk + skip, 128 - skip)
        remote(sa.at[got, :], ra.at[0, got, :], sa_s, sa_r.at[chunk], along(1)).wait_recv()
        for way, (step, land) in enumerate(((1, 1), (3, 3))):
            k = 2 * chunk + way
            copy = remote(ra.at[0, rows, :], ra.at[land, rows, :], fw_s.at[k], fw_r.at[k], along(step))
            copy.start()
            forward.append(copy)

    def make_b(k):
        if k:
            tb_copies[k - 1].wait_recv()
            spread[k] = spread_table(tbm[k, :, WB:WB + 128])
        twice = jnp.concatenate([tbm[k, :, 0:WB]] * 2, axis=0)
        at = 16 * PLACE[k]
        for chunk in range(4):
            rows = slice(128 * chunk, 128 * chunk + 128)
            sb[8 * chunk:8 * chunk + 8, at:at + 16, :] = dot(spread[k, rows, :], twice).astype(BF).reshape(8, 16, WB)

    early, late = pl.ds(0, 48), pl.ds(48, 16)

    def over_plane(src, dst, part, send, recv, back):
        def one(i, _):
            remote(src.at[i, part, :], dst.at[i, part, :], send, recv, peer(i, back)).start()
            return 0

        lax.fori_loop(1, NE, one, 0)

    def whole(src, dst, part, send, recv):
        return remote(src.at[pl.ds(1, 31), part, :], dst.at[pl.ds(1, 31), part, :], send, recv, along(1))

    make_b(0)
    send_forward(0)
    make_b(1)
    make_b(3)
    over_plane(sb, rb, early, sb_s.at[0], sb_r.at[0], False)
    send_forward(1)
    make_b(2)
    over_plane(sb, rb, late, sb_s.at[1], sb_r.at[1], False)
    rb[0] = sb[0]
    send_forward(2)
    send_forward(3)

    def into_rows(value, row, col, width):
        out = dot(perm[...], value).astype(BF)
        for arr, ref in ((0, xs), (1, gs)):
            for s in range(SEG):
                at = (4 * arr + s) * 32
                ref[row:row + 32, s * WIDE + col:s * WIDE + col + width] = out[at:at + 32]

    def multiply(row, count, col, width):
        rows = slice(row, row + count)

        def one(s, _):
            cols = pl.ds(pl.multiple_of(s * WIDE + col, 128), width)
            left = xs[rows, cols]
            acc[0, rows, :] += dot(left, wg[cols, :])
            acc[1, rows, :] += dot(left, wu[cols, :])
            acc[2, rows, :] += dot_nt(gs[rows, cols], wd[:, cols])
            return 0

        lax.fori_loop(0, SEG, one, 0)

    acc[...] = jnp.zeros_like(acc)
    for load in loads:
        load.wait()

    def sort_a(k):
        for g in range(2):
            into_rows(ra[k, 256 * g:256 * g + 256, :], 64 * PLACE[k] + 32 * g, 0, WA)

    def sort_b(k):
        at = 16 * PLACE[k]
        for g in range(2):
            into_rows(rb[16 * g:16 * g + 16, at:at + 16, :].reshape(256, WB), 64 * PLACE[k] + 32 * g, WA, WB)

    def activate(row, count):
        rows = slice(row, row + count)
        gate, up, back = acc[0, rows, :], acc[1, rows, :], acc[2, rows, :]
        sig = jax.nn.sigmoid(gate)
        act = gate * sig
        h_ref[rows, :] = (act * up).astype(BF)
        gp_ref[rows, :] = (back * up * sig * (1.0 + gate * (1.0 - sig))).astype(BF)
        up_ref[rows, :] = (back * act).astype(BF)

    sort_a(0)
    multiply(0, 64, 0, WA)
    further = []
    for chunk in range(4):
        land, step, way = (1, 1, 0) if chunk < 2 else (3, 3, 1)
        forward[2 * chunk + way].wait_recv()
        rows = pl.ds(128 * chunk, 128)
        copy = remote(ra.at[land, rows, :], ra.at[2, rows, :], f2_s.at[chunk], f2_r.at[chunk], along(step))
        copy.start()
        further.append(copy)
    for chunk in range(4):
        forward[2 * chunk + (1 if chunk < 2 else 0)].wait_recv()
    sort_a(1)
    sort_a(3)
    multiply(64, 128, 0, WA)
    whole(sb, rb, early, sb_s.at[0], sb_r.at[0]).wait_recv()
    for k in (0, 1, 3):
        sort_b(k)
    multiply(0, 192, WA, WB)
    activate(0, 192)

    def parts(k, col, width, st):
        row = 64 * PLACE[k]
        rows = slice(row, row + 64)

        def one(s, _):
            cols = pl.ds(pl.multiple_of(s * WIDE + col, 128), width)
            near = dot_nt(gp_ref[rows, :], wg[cols, :]) + dot_nt(up_ref[rows, :], wu[cols, :])
            gacc[:, cols] += jnp.sum((near * xs[rows, cols].astype(F32)).reshape(8, 8, width), axis=0)
            near = near.astype(BF)
            far = dot(h_ref[rows, :], wd[:, cols]).astype(BF)
            for g in range(2):
                st[g, pl.ds(pl.multiple_of(32 * s, 32), 32), :] = near[32 * g:32 * g + 32]
                st[g, pl.ds(pl.multiple_of(128 + 32 * s, 32), 32), :] = far[32 * g:32 * g + 32]
            return 0

        lax.fori_loop(0, SEG, one, 0)

    def parts_a(k):
        parts(k, 0, WA, st_a)
        for g in range(2):
            qa[k, 256 * g:256 * g + 256, :] = dot(perm_t[...], st_a[g]).astype(BF)

    def parts_b(k):
        parts(k, WA, WB, st_b)
        at = 16 * PLACE[k]
        for g in range(2):
            qb[16 * g:16 * g + 16, at:at + 16, :] = dot(perm_t[...], st_b[g]).astype(BF).reshape(16, 16, WB)

    gacc[...] = jnp.zeros_like(gacc)
    for k in (0, 1, 3):
        parts_b(k)
    over_plane(qb, cb, early, qb_s.at[0], qb_r.at[0], True)

    sums = {}

    def send_sum(k, chunk):
        rows = pl.ds(128 * chunk, 128)
        land, step, way = (l1, 3, 0) if k == 1 else (l3, 1, 1)
        sem = 2 * chunk + way
        copy = remote(qa.at[k, rows, :], land.at[rows, :], l_s.at[sem], l_r.at[sem], along(step))
        copy.start()
        sums[k, chunk] = copy

    def add_half(k, chunk):
        rows = slice(128 * chunk, 128 * chunk + 128)
        other = half1[rows, :] if k == 1 else half3[128 * chunk - 256:128 * chunk - 128, :]
        qa[k, rows, :] = (qa[k, rows, :].astype(F32) + other.astype(F32)).astype(BF)

    parts_a(1)
    send_sum(1, 2)
    send_sum(1, 3)
    parts_a(3)
    send_sum(3, 0)
    send_sum(3, 1)

    for copy in further:
        copy.wait_recv()
    sort_a(2)
    whole(sb, rb, late, sb_s.at[1], sb_r.at[1]).wait_recv()
    sort_b(2)
    multiply(192, 64, 0, WIDE)
    activate(192, 64)
    keep = [pltpu.make_async_copy(xs, x_hbm, out_sem.at[0]), pltpu.make_async_copy(gs, g_hbm, out_sem.at[1])]
    for copy in keep:
        copy.start()
    parts_a(2)
    low, high = pl.ds(0, 256), pl.ds(256, 256)
    halves = [
        remote(qa.at[2, low, :], half1, hf_s.at[0], hf_r.at[0], along(3)),
        remote(qa.at[2, high, :], half3, hf_s.at[1], hf_r.at[1], along(1)),
    ]
    for copy in halves:
        copy.start()
    parts_b(2)
    over_plane(qb, cb, late, qb_s.at[1], qb_r.at[1], True)
    cb[0] = qb[0]
    parts_a(0)

    term = jnp.sum(gacc[...], axis=0, keepdims=True) / gain_ref[...]
    gsend[...] = jnp.zeros_like(gsend)
    for j in range(D // 128):
        at = (j // 14) * 16 + j % 14
        gsend[at:at + 1, :] = term[:, 128 * j:128 * j + 128]

    def quarter(step):
        return gsend.at[pl.ds(pl.multiple_of(lax.rem(sx + step, 4) * 16, 16), 16), :]

    gx_copies = [remote(quarter(step), gx.at[step - 1], gx_s.at[step - 1], gx_r.at[step - 1], along(step)) for step in (1, 2, 3)]
    for copy in gx_copies:
        copy.start()
    halves[0].wait_recv()
    halves[1].wait_recv()
    add_half(1, 0)
    send_sum(1, 0)
    add_half(3, 2)
    send_sum(3, 2)
    add_half(1, 1)
    send_sum(1, 1)
    add_half(3, 3)
    send_sum(3, 3)

    def send_gain(i, _):
        remote(gpart, gl.at[i], gl_s, gl_r, peer(i, False)).start()
        return 0

    for chunk in (0, 2, 1, 3):
        if chunk == 1:
            for copy in gx_copies:
                copy.wait_recv()
            gpart[...] = gsend[pl.ds(pl.multiple_of(sx * 16, 16), 16), :] + gx[0] + gx[1] + gx[2]
            lax.fori_loop(1, NE, send_gain, 0)
            gl[0] = gpart[...]
        rows = slice(128 * chunk, 128 * chunk + 128)
        sums[1, chunk].wait_recv()
        sums[3, chunk].wait_recv()
        total = qa[0, rows, :].astype(F32) + l1[rows, :].astype(F32) + l3[rows, :].astype(F32)
        qa[0, rows, :] = total.astype(BF)

        def return_a(i, _):
            at = pl.ds(pl.multiple_of(16 * i, 16), 16)
            remote(qa.at[0, at, :], ca.at[at, :], ca_s, ca_r, peer(i, True)).start()
            return 0

        lax.fori_loop(max(8 * chunk, 1), 8 * chunk + 8, return_a, 0)
    ca[0:16, :] = qa[0, 0:16, :]

    def fold(k, value):
        out = dot_tn(spread[k], value)
        return out[0:64] + out[64:128]

    whole(qb, cb, early, qb_s.at[0], qb_r.at[0]).wait_recv()
    ys_copies = {}

    def give_back(k):
        at = 16 * PLACE[k]
        ys[k] = fold(k, cb[:, at:at + 16, :].reshape(MSG, WB)).astype(BF)
        ys_copies[k] = remote(ys.at[k], xb.at[k], ys_s.at[k - 1], ys_r.at[k - 1], along(4 - k))
        ys_copies[k].start()

    give_back(1)
    give_back(3)
    mine_b = fold(0, cb[:, 0:16, :].reshape(MSG, WB))
    whole(qb, cb, late, qb_s.at[1], qb_r.at[1]).wait_recv()
    give_back(2)
    for copy in ys_copies.values():
        copy.wait_recv()
    for k in (1, 2, 3):
        mine_b = mine_b + xb[k].astype(F32)
    for s in range(SEG):
        cols = slice(s * WIDE + WA, (s + 1) * WIDE)
        ng[:, cols] = mine_b[16 * s:16 * s + 8]
        mx[:, cols] = mine_b[16 * s + 8:16 * s + 16]
    back_rows = pl.ds(16, MSG - 16)
    remote(qa.at[0, back_rows, :], ca.at[back_rows, :], ca_s, ca_r, along(1)).wait_recv()
    mine_a = fold(0, ca[...])
    for s in range(SEG):
        cols = slice(s * WIDE, s * WIDE + WA)
        ng[:, cols] = mine_a[16 * s:16 * s + 8]
        mx[:, cols] = mine_a[16 * s + 8:16 * s + 16]

    tokens = tok_ref[...].astype(F32)
    grad = ng[...]
    mixed_ref[...] = mx[...].astype(BF)
    scaled = gain_ref[...] * grad
    inner = jnp.sum(scaled * tokens, axis=1, keepdims=True)
    tg_ref[...] = (recip * scaled - tokens * (recip * recip * recip * inner / D)).astype(BF)
    remote(gl.at[pl.ds(1, 31)], gl.at[pl.ds(1, 31)], gl_s, gl_r, along(1)).wait_recv()
    gq_ref[...] = jnp.sum(gl[...], axis=0)

    for copy in tb_copies + forward + further + halves + list(sums.values()) + list(ys_copies.values()) + gx_copies:
        copy.wait_send()
    remote(sa.at[back_rows, :], sa.at[back_rows, :], sa_s, sa_r.at[0], along(1)).wait_send()
    for n, part in enumerate((early, late)):
        whole(sb, rb, part, sb_s.at[n], sb_r.at[n]).wait_send()
        whole(qb, cb, part, qb_s.at[n], qb_r.at[n]).wait_send()
    remote(qa.at[0, back_rows, :], ca.at[back_rows, :], ca_s, ca_r, along(1)).wait_send()
    remote(gl.at[pl.ds(1, 31)], gl.at[pl.ds(1, 31)], gl_s, gl_r, along(1)).wait_send()
    for copy in keep:
        copy.wait()


def weight_grads(
    x_ref, g_ref, h_ref, gp_ref, up_ref, quarter_ref, mixed_in, tg_in,
    wg_ref, wu_ref, wd_ref, mixed_ref, tg_ref, gain_ref, turned,
):
    @pl.when(pl.program_id(0) == 0)
    def _():
        turned[...] = h_ref[...].T

    turned_x = x_ref[...].T
    wg_ref[0] = dot(turned_x, gp_ref[...]).astype(BF)
    wu_ref[0] = dot(turned_x, up_ref[...]).astype(BF)
    wd_ref[0] = dot(turned[...], g_ref[...]).astype(BF)
    mixed_ref[...] = mixed_in[...]
    tg_ref[...] = tg_in[...]

    @pl.when(pl.program_id(0) == 0)
    def _():
        first = lax.axis_index("ep") * (D // 128)
        row, lane = first // 128, lax.rem(first, 128)
        two = jnp.concatenate([quarter_ref[pl.ds(row, 1), :], quarter_ref[pl.ds(row + 1, 1), :]], axis=1)
        gain_ref[...] = pltpu.roll(two, lax.rem(256 - lane, 256), 1)[0, 0:D // 128]


def on_device(tokens, out_grad, routes, gate_fixed, ramp_step, norm_gain, w_gate, w_up, w_down):
    vmem = pl.BlockSpec(memory_space=pltpu.VMEM)
    hbm = pl.BlockSpec(memory_space=pl.ANY)
    dma = pltpu.SemaphoreType.DMA
    outs = pl.pallas_call(
        layer,
        name="layer",
        out_shape=(
            jax.ShapeDtypeStruct((TOK, D), BF),
            jax.ShapeDtypeStruct((TOK, D), BF),
            jax.ShapeDtypeStruct((16, 128), F32),
            jax.ShapeDtypeStruct((256, D), BF),
            jax.ShapeDtypeStruct((256, D), BF),
            jax.ShapeDtypeStruct((256, HID), BF),
            jax.ShapeDtypeStruct((256, HID), BF),
            jax.ShapeDtypeStruct((256, HID), BF),
        ),
        in_specs=[vmem] * 6 + [hbm] * 3,
        out_specs=(vmem, vmem, vmem, hbm, hbm, vmem, vmem, vmem),
        scratch_shapes=[
            pltpu.VMEM((D, HID), BF), pltpu.VMEM((D, HID), BF), pltpu.VMEM((HID, D), BF),
            pltpu.VMEM((128, WIDE), BF),
            pltpu.VMEM((4, 64, WB + 128), BF),
            pltpu.VMEM((4, MSG, 128), BF),
            pltpu.VMEM((256, 256), BF), pltpu.VMEM((256, 256), BF),
            pltpu.VMEM((MSG, WA), BF), pltpu.VMEM((4, MSG, WA), BF),
            pltpu.VMEM((NE, 64, WB), BF), pltpu.VMEM((NE, 64, WB), BF),
            pltpu.VMEM((256, D), BF), pltpu.VMEM((256, D), BF),
            pltpu.VMEM((3, 256, HID), F32),
            pltpu.VMEM((2, 256, WA), BF), pltpu.VMEM((2, 256, WB), BF),
            pltpu.VMEM((4, MSG, WA), BF), pltpu.VMEM((NE, 64, WB), BF),
            pltpu.VMEM((256, WA), BF), pltpu.VMEM((256, WA), BF),
            pltpu.VMEM((MSG, WA), BF), pltpu.VMEM((MSG, WA), BF),
            pltpu.VMEM((MSG, WA), BF), pltpu.VMEM((NE, 64, WB), BF),
            pltpu.VMEM((4, 64, WB), BF), pltpu.VMEM((4, 64, WB), BF),
            pltpu.VMEM((TOK, D), F32), pltpu.VMEM((TOK, D), F32),
            pltpu.VMEM((8, D), F32), pltpu.VMEM((64, 128), F32), pltpu.VMEM((3, 16, 128), F32),
            pltpu.VMEM((16, 128), F32), pltpu.VMEM((NE, 16, 128), F32),
            dma((3,)), dma((2,)), dma((3,)), dma((3,)), dma, dma((4,)), dma((8,)), dma((8,)), dma((4,)), dma((4,)), dma((2,)), dma((2,)),
            dma((2,)), dma((2,)), dma((8,)), dma((8,)), dma((2,)), dma((2,)), dma, dma, dma((3,)), dma((3,)), dma((3,)), dma((3,)), dma, dma,
        ],
        compiler_params=pltpu.CompilerParams(collective_id=0, has_side_effects=True, vmem_limit_bytes=60 * 2**20),
        cost_estimate=pl.CostEstimate(flops=8 * 10**9, bytes_accessed=20 * 10**6, transcendentals=65536),
    )(tokens, out_grad, routes, gate_fixed, ramp_step.reshape(1, NE), norm_gain.reshape(1, D), w_gate[0], w_up[0], w_down[0])
    mixed, tokens_grad, quarter, rows_x, rows_g, hidden, gate_pre, up_pre = outs
    block = 1792
    tall = pl.BlockSpec((1, block, HID), lambda i: (0, i, 0))
    wide = pl.BlockSpec((256, block), lambda i: (0, i))
    few = pl.BlockSpec((TOK, block), lambda i: (0, i))
    fixed = pl.BlockSpec((256, HID), lambda i: (0, 0))
    w_gate_grad, w_up_grad, w_down_grad, mixed, tokens_grad, gain_grad = pl.pallas_call(
        weight_grads,
        name="weight_grads",
        grid=(D // block,),
        out_shape=(
            jax.ShapeDtypeStruct((1, D, HID), BF),
            jax.ShapeDtypeStruct((1, D, HID), BF),
            jax.ShapeDtypeStruct((1, HID, D), BF),
            jax.ShapeDtypeStruct((TOK, D), BF),
            jax.ShapeDtypeStruct((TOK, D), BF),
            jax.ShapeDtypeStruct((D // 128,), F32),
        ),
        in_specs=[wide, wide, fixed, fixed, fixed, pl.BlockSpec((16, 128), lambda i: (0, 0)), few, few],
        out_specs=(tall, tall, pl.BlockSpec((1, HID, block), lambda i: (0, 0, i)), few, few, pl.BlockSpec((D // 128,), lambda i: (0,))),
        scratch_shapes=[pltpu.VMEM((HID, 256), BF)],
        compiler_params=pltpu.CompilerParams(vmem_limit_bytes=60 * 2**20),
        cost_estimate=pl.CostEstimate(flops=3 * 10**9, bytes_accessed=19 * 10**6, transcendentals=0),
    )(rows_x, rows_g, hidden, gate_pre, up_pre, quarter, mixed, tokens_grad)
    return (mixed, tokens_grad, gain_grad, w_gate_grad, w_up_grad, w_down_grad)


def solution(mesh):
    return jax.shard_map(
        on_device,
        mesh=mesh,
        in_specs=(
            P(("seq", "ep"), None),
            P(("seq", "ep"), None),
            P(("seq", "ep"), None),
            P(("seq", "ep"), None),
            P(),
            P(),
            P("ep", None, "seq"),
            P("ep", None, "seq"),
            P("ep", "seq", None),
        ),
        out_specs=(
            P(("seq", "ep"), None),
            P(("seq", "ep"), None),
            P(("seq", "ep")),
            P("ep", None, "seq"),
            P("ep", None, "seq"),
            P("ep", "seq", None),
        ),
        check_vma=False,
    )
```

```python
import functools

import jax
import jax.numpy as jnp
from jax import lax
from jax.experimental import pallas as pl
from jax.experimental.pallas import tpu as pltpu
from jax.sharding import PartitionSpec as P

MESH = pl.DeviceIdType.MESH
RAMP = 8.0
GATE_UNIT = 65536.0
NORM_EPS = 1e-06

TOK = 8
TOP = 8
PAIRS = TOK * TOP
D = 7168
HID = 256
NX, NE = 4, 32
SEG = 4
WIDE = D // SEG
WA = 1024
WB = WIDE - WA
MSG = 512
HOP, HOP_BACK = 7, 23
PLACE = {0: 0, 1: 1, 3: 2, 2: 3}
BF = jnp.bfloat16
F32 = jnp.float32


def dot(a, b):
    return lax.dot_general(a, b, (((1,), (0,)), ((), ())), preferred_element_type=F32)


def dot_nt(a, b):
    return lax.dot_general(a, b, (((1,), (1,)), ((), ())), preferred_element_type=F32)


def dot_tn(a, b):
    return lax.dot_general(a, b, (((0,), (0,)), ((), ())), preferred_element_type=F32)


def iota(shape, dim):
    return lax.broadcasted_iota(jnp.int32, shape, dim)


def pair_table(routes_ref, gate_ref, ramp_ref, z, y, c):
    rep = (iota((PAIRS, TOK), 0) // TOP == iota((PAIRS, TOK), 1)).astype(F32)
    pick = iota((PAIRS, TOP), 0) % TOP == iota((PAIRS, TOP), 1)
    pick_t = iota((TOP, PAIRS), 1) % TOP == iota((TOP, PAIRS), 0)

    def column(v):
        return jnp.sum(jnp.where(pick, dot(rep, v), 0.0), axis=1, keepdims=True)

    routes = routes_ref[...].astype(F32)
    gate = gate_ref[...]
    route_col = column(routes)
    route_row = jnp.sum(
        jnp.where(pick_t, lax.dot_general(routes, rep, (((0,), (1,)), ((), ())), preferred_element_type=F32), 0.0),
        axis=0, keepdims=True)
    gate_col = column((gate >> 8).astype(F32)) * 256.0 + column((gate & 255).astype(F32))
    same = route_col.astype(jnp.int32) == iota((PAIRS, NE), 1)
    ramp_col = jnp.sum(jnp.where(same, ramp_ref[...].astype(F32), 0.0), axis=1, keepdims=True)
    coef = gate_col / GATE_UNIT * ramp_col / RAMP
    high = coef.astype(BF).astype(F32)
    low = coef - high

    before = (route_col == route_row) & (iota((PAIRS, PAIRS), 0) < iota((PAIRS, PAIRS), 1))
    row = jnp.sum(before.astype(F32), axis=0, keepdims=True).astype(jnp.int32)
    e = route_row.astype(jnp.int32)
    way = 1 - 2 * c
    rel = ((((e >> 3) - z) * way) & 3) * 8 + (((((e >> 1) & 3) - y) * way) & 3) * 2 + (((e & 1) - c) & 1)
    slot = (rel * HOP_BACK) & 31
    place = (iota((PAIRS, PAIRS), 0) == slot * 2 + row).astype(BF)

    lane = iota((PAIRS, 128), 1)
    first, grad = lane < 64, ((lane >> 3) & 1) == 1
    mine = (iota((PAIRS, 128), 0) // TOP) == (lane & 7)
    value = jnp.where(first, jnp.where(grad, high, 1.0), jnp.where(grad, low, 0.0))
    return dot(place, jnp.where(mine, value, 0.0).astype(BF)).astype(BF)


def spread_table(pairs):
    m = iota((MSG, PAIRS), 0)
    expand = ((m >> 4) * 2 + (m & 1) == iota((MSG, PAIRS), 1)).astype(BF)
    m, lane = iota((MSG, 128), 0), iota((MSG, 128), 1)
    keep = (((m >> 2) & 3) == ((lane >> 4) & 3)) & (((m >> 1) & 1) == ((lane >> 3) & 1))
    return jnp.where(keep, dot(expand, pairs), 0.0).astype(BF)


def shuffles():
    def table(o, m):
        return (((o >> 1) & 15) * 16 + ((o >> 5) & 3) * 4 + (o >> 7) * 2 + (o & 1) == m).astype(BF)

    shape = (256, 256)
    return table(iota(shape, 0), iota(shape, 1)), table(iota(shape, 1), iota(shape, 0))


def layer(
    tok_ref, og_ref, routes_ref, gate_ref, ramp_ref, gain_ref, wg_hbm, wu_hbm, wd_hbm,
    mixed_ref, tg_ref, gq_ref, x_hbm, g_hbm, h_ref, gp_ref, up_ref,
    wg, wu, wd, tab, tbm, spread, perm, perm_t, sa, ra, sb, rb, xs, gs, acc, st_a, st_b,
    qa, qb, half1, half3, l1, l3, ca, cb, ys, xb, ng, mx, gacc, gsend, gx, gpart, gl,
    w_sem, out_sem, tb_s, tb_r, sa_s, sa_r, fw_s, fw_r, f2_s, f2_r, sb_s, sb_r,
    hf_s, hf_r, l_s, l_r, qb_s, qb_r, ca_s, ca_r, ys_s, ys_r, gx_s, gx_r, gl_s, gl_r,
):
    sx = lax.axis_index("seq")
    me = lax.axis_index("ep")
    z, y, c = me // 8, lax.rem(me // 2, 4), lax.rem(me, 2)

    def along(step):
        return {"seq": lax.rem(sx + step, 4)}

    def peer(i, back):
        b = lax.rem(i * HOP, 32)
        dz, dy, dc = b // 8, lax.rem(b // 2, 4), lax.rem(b, 2)
        way = 1 - 2 * lax.rem(c + dc + 1, 2) if back else 1 - 2 * c
        return {"ep": lax.rem(z + 4 + way * dz, 4) * 8 + lax.rem(y + 4 + way * dy, 4) * 2 + lax.rem(c + dc, 2)}

    def remote(src, dst, send, recv, to):
        return pltpu.make_async_remote_copy(src, dst, send, recv, device_id=to, device_id_type=MESH)

    barrier = pltpu.get_barrier_semaphore()
    for step in (1, 2, 3):
        pl.semaphore_signal(barrier, inc=1, device_id=along(step), device_id_type=MESH)

    def greet(i, _):
        pl.semaphore_signal(barrier, inc=1, device_id=peer(i, False), device_id_type=MESH)
        return 0

    lax.fori_loop(1, NE, greet, 0)

    loads = [pltpu.make_async_copy(a, b, w_sem.at[i]) for i, (a, b) in enumerate(((wg_hbm, wg), (wu_hbm, wu), (wd_hbm, wd)))]
    for load in loads:
        load.start()

    tokens = tok_ref[...].astype(F32)
    recip = lax.rsqrt(jnp.sum(tokens * tokens, axis=1, keepdims=True) / D + NORM_EPS)
    for s in range(SEG):
        cols = slice(s * WIDE, (s + 1) * WIDE)
        normed = tok_ref[:, cols].astype(F32) * recip * gain_ref[:, cols]
        both = jnp.concatenate([normed, og_ref[:, cols].astype(F32)], axis=0).astype(BF)
        tab[16 * s:16 * s + 16, :] = both
        tab[64 + 16 * s:80 + 16 * s, :] = both
    pairs = pair_table(routes_ref, gate_ref, ramp_ref, z, y, c)
    tbm[0, :, 0:WB] = tab[0:64, WA:WIDE]
    tbm[0, :, WB:WB + 128] = pairs
    pl.semaphore_wait(barrier, 34)

    tb_copies = [remote(tbm.at[0], tbm.at[step], tb_s.at[step - 1], tb_r.at[step - 1], along(step)) for step in (1, 2, 3)]
    for copy in tb_copies:
        copy.start()

    spread[0] = spread_table(pairs)
    for chunk in range(4):
        rows = slice(128 * chunk, 128 * chunk + 128)
        sa[rows, :] = dot(spread[0, rows, :], tab[:, 0:WA]).astype(BF)

        def send_a(i, _, chunk=chunk):
            at = pl.ds(pl.multiple_of(16 * i, 16), 16)
            remote(sa.at[at, :], ra.at[0, at, :], sa_s, sa_r.at[chunk], peer(i, False)).start()
            return 0

        lax.fori_loop(max(8 * chunk, 1), 8 * chunk + 8, send_a, 0)
    ra[0, 0:16, :] = sa[0:16, :]
    p, p_t = shuffles()
    perm[...] = p
    perm_t[...] = p_t

    forward = []

    def send_forward(chunk):
        rows = pl.ds(128 * chunk, 128)
        skip = 16 if chunk == 0 else 0
        got = pl.ds(128 * chunk + skip, 128 - skip)
        remote(sa.at[got, :], ra.at[0, got, :], sa_s, sa_r.at[chunk], along(1)).wait_recv()
        for way, (step, land) in enumerate(((1, 1), (3, 3))):
            k = 2 * chunk + way
            copy = remote(ra.at[0, rows, :], ra.at[land, rows, :], fw_s.at[k], fw_r.at[k], along(step))
            copy.start()
            forward.append(copy)

    def make_b(k):
        if k:
            tb_copies[k - 1].wait_recv()
            spread[k] = spread_table(tbm[k, :, WB:WB + 128])
        twice = jnp.concatenate([tbm[k, :, 0:WB]] * 2, axis=0)
        at = 16 * PLACE[k]
        for chunk in range(4):
            rows = slice(128 * chunk, 128 * chunk + 128)
            sb[8 * chunk:8 * chunk + 8, at:at + 16, :] = dot(spread[k, rows, :], twice).astype(BF).reshape(8, 16, WB)

    early, late = pl.ds(0, 48), pl.ds(48, 16)

    def over_plane(src, dst, part, send, recv, back):
        def one(i, _):
            remote(src.at[i, part, :], dst.at[i, part, :], send, recv, peer(i, back)).start()
            return 0

        lax.fori_loop(1, NE, one, 0)

    def whole(src, dst, part, send, recv):
        return remote(src.at[pl.ds(1, 31), part, :], dst.at[pl.ds(1, 31), part, :], send, recv, along(1))

    make_b(0)
    send_forward(0)
    make_b(1)
    make_b(3)
    over_plane(sb, rb, early, sb_s.at[0], sb_r.at[0], False)
    send_forward(1)
    make_b(2)
    over_plane(sb, rb, late, sb_s.at[1], sb_r.at[1], False)
    rb[0] = sb[0]
    send_forward(2)
    send_forward(3)

    def into_rows(value, row, col, width):
        out = dot(perm[...], value).astype(BF)
        for arr, ref in ((0, xs), (1, gs)):
            for s in range(SEG):
                at = (4 * arr + s) * 32
                ref[row:row + 32, s * WIDE + col:s * WIDE + col + width] = out[at:at + 32]

    def multiply(row, count, col, width):
        rows = slice(row, row + count)

        def one(s, _):
            cols = pl.ds(pl.multiple_of(s * WIDE + col, 128), width)
            left = xs[rows, cols]
            acc[0, rows, :] += dot(left, wg[cols, :])
            acc[1, rows, :] += dot(left, wu[cols, :])
            acc[2, rows, :] += dot_nt(gs[rows, cols], wd[:, cols])
            return 0

        lax.fori_loop(0, SEG, one, 0)

    acc[...] = jnp.zeros_like(acc)
    for load in loads:
        load.wait()

    def sort_a(k):
        for g in range(2):
            into_rows(ra[k, 256 * g:256 * g + 256, :], 64 * PLACE[k] + 32 * g, 0, WA)

    def sort_b(k):
        at = 16 * PLACE[k]
        for g in range(2):
            into_rows(rb[16 * g:16 * g + 16, at:at + 16, :].reshape(256, WB), 64 * PLACE[k] + 32 * g, WA, WB)

    def activate(row, count):
        rows = slice(row, row + count)
        gate, up, back = acc[0, rows, :], acc[1, rows, :], acc[2, rows, :]
        sig = jax.nn.sigmoid(gate)
        act = gate * sig
        h_ref[rows, :] = (act * up).astype(BF)
        gp_ref[rows, :] = (back * up * sig * (1.0 + gate * (1.0 - sig))).astype(BF)
        up_ref[rows, :] = (back * act).astype(BF)

    sort_a(0)
    multiply(0, 64, 0, WA)
    further = []
    for chunk in range(4):
        land, step, way = (1, 1, 0) if chunk < 2 else (3, 3, 1)
        forward[2 * chunk + way].wait_recv()
        rows = pl.ds(128 * chunk, 128)
        copy = remote(ra.at[land, rows, :], ra.at[2, rows, :], f2_s.at[chunk], f2_r.at[chunk], along(step))
        copy.start()
        further.append(copy)
    for chunk in range(4):
        forward[2 * chunk + (1 if chunk < 2 else 0)].wait_recv()
    sort_a(1)
    sort_a(3)
    multiply(64, 128, 0, WA)
    whole(sb, rb, early, sb_s.at[0], sb_r.at[0]).wait_recv()
    for k in (0, 1, 3):
        sort_b(k)
    multiply(0, 192, WA, WB)
    activate(0, 192)

    def parts(k, col, width, st):
        row = 64 * PLACE[k]
        rows = slice(row, row + 64)

        def one(s, _):
            cols = pl.ds(pl.multiple_of(s * WIDE + col, 128), width)
            near = dot_nt(gp_ref[rows, :], wg[cols, :]) + dot_nt(up_ref[rows, :], wu[cols, :])
            gacc[:, cols] += jnp.sum((near * xs[rows, cols].astype(F32)).reshape(8, 8, width), axis=0)
            near = near.astype(BF)
            far = dot(h_ref[rows, :], wd[:, cols]).astype(BF)
            for g in range(2):
                st[g, pl.ds(pl.multiple_of(32 * s, 32), 32), :] = near[32 * g:32 * g + 32]
                st[g, pl.ds(pl.multiple_of(128 + 32 * s, 32), 32), :] = far[32 * g:32 * g + 32]
            return 0

        lax.fori_loop(0, SEG, one, 0)

    def parts_a(k):
        parts(k, 0, WA, st_a)
        for g in range(2):
            qa[k, 256 * g:256 * g + 256, :] = dot(perm_t[...], st_a[g]).astype(BF)

    def parts_b(k):
        parts(k, WA, WB, st_b)
        at = 16 * PLACE[k]
        for g in range(2):
            qb[16 * g:16 * g + 16, at:at + 16, :] = dot(perm_t[...], st_b[g]).astype(BF).reshape(16, 16, WB)

    gacc[...] = jnp.zeros_like(gacc)
    for k in (0, 1, 3):
        parts_b(k)
    over_plane(qb, cb, early, qb_s.at[0], qb_r.at[0], True)

    sums = {}

    def send_sum(k, chunk):
        rows = pl.ds(128 * chunk, 128)
        land, step, way = (l1, 3, 0) if k == 1 else (l3, 1, 1)
        sem = 2 * chunk + way
        copy = remote(qa.at[k, rows, :], land.at[rows, :], l_s.at[sem], l_r.at[sem], along(step))
        copy.start()
        sums[k, chunk] = copy

    def add_half(k, chunk):
        rows = slice(128 * chunk, 128 * chunk + 128)
        other = half1[rows, :] if k == 1 else half3[128 * chunk - 256:128 * chunk - 128, :]
        qa[k, rows, :] = (qa[k, rows, :].astype(F32) + other.astype(F32)).astype(BF)

    parts_a(1)
    send_sum(1, 2)
    send_sum(1, 3)
    parts_a(3)
    send_sum(3, 0)
    send_sum(3, 1)

    for copy in further:
        copy.wait_recv()
    sort_a(2)
    whole(sb, rb, late, sb_s.at[1], sb_r.at[1]).wait_recv()
    sort_b(2)
    multiply(192, 64, 0, WIDE)
    activate(192, 64)
    keep = [pltpu.make_async_copy(xs, x_hbm, out_sem.at[0]), pltpu.make_async_copy(gs, g_hbm, out_sem.at[1])]
    for copy in keep:
        copy.start()
    parts_a(2)
    low, high = pl.ds(0, 256), pl.ds(256, 256)
    halves = [
        remote(qa.at[2, low, :], half1, hf_s.at[0], hf_r.at[0], along(3)),
        remote(qa.at[2, high, :], half3, hf_s.at[1], hf_r.at[1], along(1)),
    ]
    for copy in halves:
        copy.start()
    parts_b(2)
    over_plane(qb, cb, late, qb_s.at[1], qb_r.at[1], True)
    cb[0] = qb[0]
    parts_a(0)

    term = jnp.sum(gacc[...], axis=0, keepdims=True) / gain_ref[...]
    gsend[...] = jnp.zeros_like(gsend)
    for j in range(D // 128):
        at = (j // 14) * 16 + j % 14
        gsend[at:at + 1, :] = term[:, 128 * j:128 * j + 128]

    def quarter(step):
        return gsend.at[pl.ds(pl.multiple_of(lax.rem(sx + step, 4) * 16, 16), 16), :]

    gx_copies = [remote(quarter(step), gx.at[step - 1], gx_s.at[step - 1], gx_r.at[step - 1], along(step)) for step in (1, 2, 3)]
    for copy in gx_copies:
        copy.start()
    halves[0].wait_recv()
    halves[1].wait_recv()
    add_half(1, 0)
    send_sum(1, 0)
    add_half(3, 2)
    send_sum(3, 2)
    add_half(1, 1)
    send_sum(1, 1)
    add_half(3, 3)
    send_sum(3, 3)

    def send_gain(i, _):
        remote(gpart, gl.at[i], gl_s, gl_r, peer(i, False)).start()
        return 0

    for chunk in (0, 2, 1, 3):
        if chunk == 1:
            for copy in gx_copies:
                copy.wait_recv()
            gpart[...] = gsend[pl.ds(pl.multiple_of(sx * 16, 16), 16), :] + gx[0] + gx[1] + gx[2]
            lax.fori_loop(1, NE, send_gain, 0)
            gl[0] = gpart[...]
        rows = slice(128 * chunk, 128 * chunk + 128)
        sums[1, chunk].wait_recv()
        sums[3, chunk].wait_recv()
        total = qa[0, rows, :].astype(F32) + l1[rows, :].astype(F32) + l3[rows, :].astype(F32)
        qa[0, rows, :] = total.astype(BF)

        def return_a(i, _):
            at = pl.ds(pl.multiple_of(16 * i, 16), 16)
            remote(qa.at[0, at, :], ca.at[at, :], ca_s, ca_r, peer(i, True)).start()
            return 0

        lax.fori_loop(max(8 * chunk, 1), 8 * chunk + 8, return_a, 0)
    ca[0:16, :] = qa[0, 0:16, :]

    def fold(k, value):
        out = dot_tn(spread[k], value)
        return out[0:64] + out[64:128]

    whole(qb, cb, early, qb_s.at[0], qb_r.at[0]).wait_recv()
    ys_copies = {}

    def give_back(k):
        at = 16 * PLACE[k]
        ys[k] = fold(k, cb[:, at:at + 16, :].reshape(MSG, WB)).astype(BF)
        ys_copies[k] = remote(ys.at[k], xb.at[k], ys_s.at[k - 1], ys_r.at[k - 1], along(4 - k))
        ys_copies[k].start()

    give_back(1)
    give_back(3)
    mine_b = fold(0, cb[:, 0:16, :].reshape(MSG, WB))
    whole(qb, cb, late, qb_s.at[1], qb_r.at[1]).wait_recv()
    give_back(2)
    for copy in ys_copies.values():
        copy.wait_recv()
    for k in (1, 2, 3):
        mine_b = mine_b + xb[k].astype(F32)
    for s in range(SEG):
        cols = slice(s * WIDE + WA, (s + 1) * WIDE)
        ng[:, cols] = mine_b[16 * s:16 * s + 8]
        mx[:, cols] = mine_b[16 * s + 8:16 * s + 16]
    back_rows = pl.ds(16, MSG - 16)
    remote(qa.at[0, back_rows, :], ca.at[back_rows, :], ca_s, ca_r, along(1)).wait_recv()
    mine_a = fold(0, ca[...])
    for s in range(SEG):
        cols = slice(s * WIDE, s * WIDE + WA)
        ng[:, cols] = mine_a[16 * s:16 * s + 8]
        mx[:, cols] = mine_a[16 * s + 8:16 * s + 16]

    tokens = tok_ref[...].astype(F32)
    grad = ng[...]
    mixed_ref[...] = mx[...].astype(BF)
    scaled = gain_ref[...] * grad
    inner = jnp.sum(scaled * tokens, axis=1, keepdims=True)
    tg_ref[...] = (recip * scaled - tokens * (recip * recip * recip * inner / D)).astype(BF)
    remote(gl.at[pl.ds(1, 31)], gl.at[pl.ds(1, 31)], gl_s, gl_r, along(1)).wait_recv()
    gq_ref[...] = jnp.sum(gl[...], axis=0)

    for copy in tb_copies + forward + further + halves + list(sums.values()) + list(ys_copies.values()) + gx_copies:
        copy.wait_send()
    remote(sa.at[back_rows, :], sa.at[back_rows, :], sa_s, sa_r.at[0], along(1)).wait_send()
    for n, part in enumerate((early, late)):
        whole(sb, rb, part, sb_s.at[n], sb_r.at[n]).wait_send()
        whole(qb, cb, part, qb_s.at[n], qb_r.at[n]).wait_send()
    remote(qa.at[0, back_rows, :], ca.at[back_rows, :], ca_s, ca_r, along(1)).wait_send()
    remote(gl.at[pl.ds(1, 31)], gl.at[pl.ds(1, 31)], gl_s, gl_r, along(1)).wait_send()
    for copy in keep:
        copy.wait()


def weight_grads(
    x_ref, g_ref, h_ref, gp_ref, up_ref, quarter_ref, mixed_in, tg_in,
    wg_ref, wu_ref, wd_ref, mixed_ref, tg_ref, gain_ref, turned,
):
    @pl.when(pl.program_id(0) == 0)
    def _():
        turned[...] = h_ref[...].T

    turned_x = x_ref[...].T
    wg_ref[0] = dot(turned_x, gp_ref[...]).astype(BF)
    wu_ref[0] = dot(turned_x, up_ref[...]).astype(BF)
    wd_ref[0] = dot(turned[...], g_ref[...]).astype(BF)
    mixed_ref[...] = mixed_in[...]
    tg_ref[...] = tg_in[...]

    @pl.when(pl.program_id(0) == 0)
    def _():
        first = lax.axis_index("ep") * (D // 128)
        row, lane = first // 128, lax.rem(first, 128)
        two = jnp.concatenate([quarter_ref[pl.ds(row, 1), :], quarter_ref[pl.ds(row + 1, 1), :]], axis=1)
        gain_ref[...] = pltpu.roll(two, lax.rem(256 - lane, 256), 1)[0, 0:D // 128]


def on_device(tokens, out_grad, routes, gate_fixed, ramp_step, norm_gain, w_gate, w_up, w_down):
    vmem = pl.BlockSpec(memory_space=pltpu.VMEM)
    hbm = pl.BlockSpec(memory_space=pl.ANY)
    dma = pltpu.SemaphoreType.DMA
    outs = pl.pallas_call(
        layer,
        name="layer",
        out_shape=(
            jax.ShapeDtypeStruct((TOK, D), BF),
            jax.ShapeDtypeStruct((TOK, D), BF),
            jax.ShapeDtypeStruct((16, 128), F32),
            jax.ShapeDtypeStruct((256, D), BF),
            jax.ShapeDtypeStruct((256, D), BF),
            jax.ShapeDtypeStruct((256, HID), BF),
            jax.ShapeDtypeStruct((256, HID), BF),
            jax.ShapeDtypeStruct((256, HID), BF),
        ),
        in_specs=[vmem] * 6 + [hbm] * 3,
        out_specs=(vmem, vmem, vmem, hbm, hbm, vmem, vmem, vmem),
        scratch_shapes=[
            pltpu.VMEM((D, HID), BF), pltpu.VMEM((D, HID), BF), pltpu.VMEM((HID, D), BF),
            pltpu.VMEM((128, WIDE), BF),
            pltpu.VMEM((4, 64, WB + 128), BF),
            pltpu.VMEM((4, MSG, 128), BF),
            pltpu.VMEM((256, 256), BF), pltpu.VMEM((256, 256), BF),
            pltpu.VMEM((MSG, WA), BF), pltpu.VMEM((4, MSG, WA), BF),
            pltpu.VMEM((NE, 64, WB), BF), pltpu.VMEM((NE, 64, WB), BF),
            pltpu.VMEM((256, D), BF), pltpu.VMEM((256, D), BF),
            pltpu.VMEM((3, 256, HID), F32),
            pltpu.VMEM((2, 256, WA), BF), pltpu.VMEM((2, 256, WB), BF),
            pltpu.VMEM((4, MSG, WA), BF), pltpu.VMEM((NE, 64, WB), BF),
            pltpu.VMEM((256, WA), BF), pltpu.VMEM((256, WA), BF),
            pltpu.VMEM((MSG, WA), BF), pltpu.VMEM((MSG, WA), BF),
            pltpu.VMEM((MSG, WA), BF), pltpu.VMEM((NE, 64, WB), BF),
            pltpu.VMEM((4, 64, WB), BF), pltpu.VMEM((4, 64, WB), BF),
            pltpu.VMEM((TOK, D), F32), pltpu.VMEM((TOK, D), F32),
            pltpu.VMEM((8, D), F32), pltpu.VMEM((64, 128), F32), pltpu.VMEM((3, 16, 128), F32),
            pltpu.VMEM((16, 128), F32), pltpu.VMEM((NE, 16, 128), F32),
            dma((3,)), dma((2,)), dma((3,)), dma((3,)), dma, dma((4,)), dma((8,)), dma((8,)), dma((4,)), dma((4,)), dma((2,)), dma((2,)),
            dma((2,)), dma((2,)), dma((8,)), dma((8,)), dma((2,)), dma((2,)), dma, dma, dma((3,)), dma((3,)), dma((3,)), dma((3,)), dma, dma,
        ],
        compiler_params=pltpu.CompilerParams(collective_id=0, has_side_effects=True, vmem_limit_bytes=60 * 2**20),
        cost_estimate=pl.CostEstimate(flops=8 * 10**9, bytes_accessed=20 * 10**6, transcendentals=65536),
    )(tokens, out_grad, routes, gate_fixed, ramp_step.reshape(1, NE), norm_gain.reshape(1, D), w_gate[0], w_up[0], w_down[0])
    mixed, tokens_grad, quarter, rows_x, rows_g, hidden, gate_pre, up_pre = outs
    block = 3584
    tall = pl.BlockSpec((1, block, HID), lambda i: (0, i, 0))
    wide = pl.BlockSpec((256, block), lambda i: (0, i))
    few = pl.BlockSpec((TOK, block), lambda i: (0, i))
    fixed = pl.BlockSpec((256, HID), lambda i: (0, 0))
    w_gate_grad, w_up_grad, w_down_grad, mixed, tokens_grad, gain_grad = pl.pallas_call(
        weight_grads,
        name="weight_grads",
        grid=(D // block,),
        out_shape=(
            jax.ShapeDtypeStruct((1, D, HID), BF),
            jax.ShapeDtypeStruct((1, D, HID), BF),
            jax.ShapeDtypeStruct((1, HID, D), BF),
            jax.ShapeDtypeStruct((TOK, D), BF),
            jax.ShapeDtypeStruct((TOK, D), BF),
            jax.ShapeDtypeStruct((D // 128,), F32),
        ),
        in_specs=[wide, wide, fixed, fixed, fixed, pl.BlockSpec((16, 128), lambda i: (0, 0)), few, few],
        out_specs=(tall, tall, pl.BlockSpec((1, HID, block), lambda i: (0, 0, i)), few, few, pl.BlockSpec((D // 128,), lambda i: (0,))),
        scratch_shapes=[pltpu.VMEM((HID, 256), BF)],
        compiler_params=pltpu.CompilerParams(vmem_limit_bytes=60 * 2**20),
        cost_estimate=pl.CostEstimate(flops=3 * 10**9, bytes_accessed=19 * 10**6, transcendentals=0),
    )(rows_x, rows_g, hidden, gate_pre, up_pre, quarter, mixed, tokens_grad)
    return (mixed, tokens_grad, gain_grad, w_gate_grad, w_up_grad, w_down_grad)


def solution(mesh):
    return jax.shard_map(
        on_device,
        mesh=mesh,
        in_specs=(
            P(("seq", "ep"), None),
            P(("seq", "ep"), None),
            P(("seq", "ep"), None),
            P(("seq", "ep"), None),
            P(),
            P(),
            P("ep", None, "seq"),
            P("ep", None, "seq"),
            P("ep", "seq", None),
        ),
        out_specs=(
            P(("seq", "ep"), None),
            P(("seq", "ep"), None),
            P(("seq", "ep")),
            P("ep", None, "seq"),
            P("ep", None, "seq"),
            P("ep", "seq", None),
        ),
        check_vma=False,
    )
```

```python
import functools

import jax
import jax.numpy as jnp
from jax import lax
from jax.experimental import pallas as pl
from jax.experimental.pallas import tpu as pltpu
from jax.sharding import PartitionSpec as P

MESH = pl.DeviceIdType.MESH
RAMP = 8.0
GATE_UNIT = 65536.0
NORM_EPS = 1e-06

TOK = 8
TOP = 8
PAIRS = TOK * TOP
D = 7168
HID = 256
NX, NE = 4, 32
SEG = 4
WIDE = D // SEG
WA = 1024
WB = WIDE - WA
MSG = 512
HOP, HOP_BACK = 7, 23
PLACE = {0: 0, 1: 1, 3: 2, 2: 3}
BF = jnp.bfloat16
F32 = jnp.float32


def dot(a, b):
    return lax.dot_general(a, b, (((1,), (0,)), ((), ())), preferred_element_type=F32)


def dot_nt(a, b):
    return lax.dot_general(a, b, (((1,), (1,)), ((), ())), preferred_element_type=F32)


def dot_tn(a, b):
    return lax.dot_general(a, b, (((0,), (0,)), ((), ())), preferred_element_type=F32)


def iota(shape, dim):
    return lax.broadcasted_iota(jnp.int32, shape, dim)


def pair_table(routes_ref, gate_ref, ramp_ref, z, y, c):
    rep = (iota((PAIRS, TOK), 0) // TOP == iota((PAIRS, TOK), 1)).astype(F32)
    pick = iota((PAIRS, TOP), 0) % TOP == iota((PAIRS, TOP), 1)
    pick_t = iota((TOP, PAIRS), 1) % TOP == iota((TOP, PAIRS), 0)

    def column(v):
        return jnp.sum(jnp.where(pick, dot(rep, v), 0.0), axis=1, keepdims=True)

    routes = routes_ref[...].astype(F32)
    gate = gate_ref[...]
    route_col = column(routes)
    route_row = jnp.sum(
        jnp.where(pick_t, lax.dot_general(routes, rep, (((0,), (1,)), ((), ())), preferred_element_type=F32), 0.0),
        axis=0, keepdims=True)
    gate_col = column((gate >> 8).astype(F32)) * 256.0 + column((gate & 255).astype(F32))
    same = route_col.astype(jnp.int32) == iota((PAIRS, NE), 1)
    ramp_col = jnp.sum(jnp.where(same, ramp_ref[...].astype(F32), 0.0), axis=1, keepdims=True)
    coef = gate_col / GATE_UNIT * ramp_col / RAMP
    high = coef.astype(BF).astype(F32)
    low = coef - high

    before = (route_col == route_row) & (iota((PAIRS, PAIRS), 0) < iota((PAIRS, PAIRS), 1))
    row = jnp.sum(before.astype(F32), axis=0, keepdims=True).astype(jnp.int32)
    e = route_row.astype(jnp.int32)
    way = 1 - 2 * c
    rel = ((((e >> 3) - z) * way) & 3) * 8 + (((((e >> 1) & 3) - y) * way) & 3) * 2 + (((e & 1) - c) & 1)
    slot = (rel * HOP_BACK) & 31
    place = (iota((PAIRS, PAIRS), 0) == slot * 2 + row).astype(BF)

    lane = iota((PAIRS, 128), 1)
    first, grad = lane < 64, ((lane >> 3) & 1) == 1
    mine = (iota((PAIRS, 128), 0) // TOP) == (lane & 7)
    value = jnp.where(first, jnp.where(grad, high, 1.0), jnp.where(grad, low, 0.0))
    return dot(place, jnp.where(mine, value, 0.0).astype(BF)).astype(BF)


def spread_table(pairs):
    m = iota((MSG, PAIRS), 0)
    expand = ((m >> 4) * 2 + (m & 1) == iota((MSG, PAIRS), 1)).astype(BF)
    m, lane = iota((MSG, 128), 0), iota((MSG, 128), 1)
    keep = (((m >> 2) & 3) == ((lane >> 4) & 3)) & (((m >> 1) & 1) == ((lane >> 3) & 1))
    return jnp.where(keep, dot(expand, pairs), 0.0).astype(BF)


def shuffles():
    def table(o, m):
        return (((o >> 1) & 15) * 16 + ((o >> 5) & 3) * 4 + (o >> 7) * 2 + (o & 1) == m).astype(BF)

    shape = (256, 256)
    return table(iota(shape, 0), iota(shape, 1)), table(iota(shape, 1), iota(shape, 0))


def layer(
    tok_ref, og_ref, routes_ref, gate_ref, ramp_ref, gain_ref, wg_hbm, wu_hbm, wd_hbm,
    mixed_ref, tg_ref, gq_ref, x_hbm, g_hbm, h_ref, gp_ref, up_ref,
    wg, wu, wd, tab, tbm, spread, perm, perm_t, sa, ra, sb, rb, xs, gs, acc, st_a, st_b,
    qa, qb, half1, half3, l1, l3, ca, cb, ys, xb, ng, mx, gacc, gsend, gx, gpart, gl,
    w_sem, out_sem, tb_s, tb_r, sa_s, sa_r, fw_s, fw_r, f2_s, f2_r, sb_s, sb_r,
    hf_s, hf_r, l_s, l_r, qb_s, qb_r, ca_s, ca_r, ys_s, ys_r, gx_s, gx_r, gl_s, gl_r,
):
    sx = lax.axis_index("seq")
    me = lax.axis_index("ep")
    z, y, c = me // 8, lax.rem(me // 2, 4), lax.rem(me, 2)

    def along(step):
        return {"seq": lax.rem(sx + step, 4)}

    way = 1 - 2 * c
    planes = [lax.rem(z + 4 + way * d, 4) * 8 for d in range(4)]
    lines = [lax.rem(y + 4 + way * d, 4) * 2 for d in range(4)]
    cores = [c, 1 - c]

    def peer(i, back):
        b = i * HOP % 32
        dz, dy, dc = b // 8, b // 2 % 4, b % 2
        if back and dc == 0:
            dz, dy = -dz % 4, -dy % 4
        return {"ep": planes[dz] + lines[dy] + cores[dc]}

    def remote(src, dst, send, recv, to):
        return pltpu.make_async_remote_copy(src, dst, send, recv, device_id=to, device_id_type=MESH)

    barrier = pltpu.get_barrier_semaphore()
    for step in (1, 2, 3):
        pl.semaphore_signal(barrier, inc=1, device_id=along(step), device_id_type=MESH)

    def greet(i, _):
        pl.semaphore_signal(barrier, inc=1, device_id=peer(i, False), device_id_type=MESH)
        return 0

    for i in range(1, NE):
        greet(i, 0)

    loads = [pltpu.make_async_copy(a, b, w_sem.at[i]) for i, (a, b) in enumerate(((wg_hbm, wg), (wu_hbm, wu), (wd_hbm, wd)))]
    for load in loads:
        load.start()

    tokens = tok_ref[...].astype(F32)
    recip = lax.rsqrt(jnp.sum(tokens * tokens, axis=1, keepdims=True) / D + NORM_EPS)
    for s in range(SEG):
        cols = slice(s * WIDE, (s + 1) * WIDE)
        normed = tok_ref[:, cols].astype(F32) * recip * gain_ref[:, cols]
        both = jnp.concatenate([normed, og_ref[:, cols].astype(F32)], axis=0).astype(BF)
        tab[16 * s:16 * s + 16, :] = both
        tab[64 + 16 * s:80 + 16 * s, :] = both
    pairs = pair_table(routes_ref, gate_ref, ramp_ref, z, y, c)
    tbm[0, :, 0:WB] = tab[0:64, WA:WIDE]
    tbm[0, :, WB:WB + 128] = pairs
    pl.semaphore_wait(barrier, 34)

    tb_copies = [remote(tbm.at[0], tbm.at[step], tb_s.at[step - 1], tb_r.at[step - 1], along(step)) for step in (1, 2, 3)]
    for copy in tb_copies:
        copy.start()

    spread[0] = spread_table(pairs)
    for chunk in range(4):
        rows = slice(128 * chunk, 128 * chunk + 128)
        sa[rows, :] = dot(spread[0, rows, :], tab[:, 0:WA]).astype(BF)

        def send_a(i, _, chunk=chunk):
            at = pl.ds(16 * i, 16)
            remote(sa.at[at, :], ra.at[0, at, :], sa_s, sa_r.at[chunk], peer(i, False)).start()
            return 0

        for i in range(max(8 * chunk, 1), 8 * chunk + 8):
            send_a(i, 0)
    ra[0, 0:16, :] = sa[0:16, :]
    p, p_t = shuffles()
    perm[...] = p
    perm_t[...] = p_t

    forward = []

    def send_forward(chunk):
        rows = pl.ds(128 * chunk, 128)
        skip = 16 if chunk == 0 else 0
        got = pl.ds(128 * chunk + skip, 128 - skip)
        remote(sa.at[got, :], ra.at[0, got, :], sa_s, sa_r.at[chunk], along(1)).wait_recv()
        for way, (step, land) in enumerate(((1, 1), (3, 3))):
            k = 2 * chunk + way
            copy = remote(ra.at[0, rows, :], ra.at[land, rows, :], fw_s.at[k], fw_r.at[k], along(step))
            copy.start()
            forward.append(copy)

    def make_b(k):
        if k:
            tb_copies[k - 1].wait_recv()
            spread[k] = spread_table(tbm[k, :, WB:WB + 128])
        twice = jnp.concatenate([tbm[k, :, 0:WB]] * 2, axis=0)
        at = 16 * PLACE[k]
        for chunk in range(4):
            rows = slice(128 * chunk, 128 * chunk + 128)
            sb[8 * chunk:8 * chunk + 8, at:at + 16, :] = dot(spread[k, rows, :], twice).astype(BF).reshape(8, 16, WB)

    early, late = pl.ds(0, 48), pl.ds(48, 16)

    def over_plane(src, dst, part, send, recv, back):
        def one(i, _):
            remote(src.at[i, part, :], dst.at[i, part, :], send, recv, peer(i, back)).start()
            return 0

        for i in range(1, NE):
            one(i, 0)

    def whole(src, dst, part, send, recv):
        return remote(src.at[pl.ds(1, 31), part, :], dst.at[pl.ds(1, 31), part, :], send, recv, along(1))

    make_b(0)
    send_forward(0)
    make_b(1)
    make_b(3)
    over_plane(sb, rb, early, sb_s.at[0], sb_r.at[0], False)
    send_forward(1)
    make_b(2)
    over_plane(sb, rb, late, sb_s.at[1], sb_r.at[1], False)
    rb[0] = sb[0]
    send_forward(2)
    send_forward(3)

    def into_rows(value, row, col, width):
        out = dot(perm[...], value).astype(BF)
        for arr, ref in ((0, xs), (1, gs)):
            for s in range(SEG):
                at = (4 * arr + s) * 32
                ref[row:row + 32, s * WIDE + col:s * WIDE + col + width] = out[at:at + 32]

    def multiply(row, count, col, width):
        rows = slice(row, row + count)

        def one(s, _):
            cols = pl.ds(pl.multiple_of(s * WIDE + col, 128), width)
            left = xs[rows, cols]
            acc[0, rows, :] += dot(left, wg[cols, :])
            acc[1, rows, :] += dot(left, wu[cols, :])
            acc[2, rows, :] += dot_nt(gs[rows, cols], wd[:, cols])
            return 0

        lax.fori_loop(0, SEG, one, 0)

    acc[...] = jnp.zeros_like(acc)
    for load in loads:
        load.wait()

    def sort_a(k):
        for g in range(2):
            into_rows(ra[k, 256 * g:256 * g + 256, :], 64 * PLACE[k] + 32 * g, 0, WA)

    def sort_b(k):
        at = 16 * PLACE[k]
        for g in range(2):
            into_rows(rb[16 * g:16 * g + 16, at:at + 16, :].reshape(256, WB), 64 * PLACE[k] + 32 * g, WA, WB)

    def activate(row, count):
        rows = slice(row, row + count)
        gate, up, back = acc[0, rows, :], acc[1, rows, :], acc[2, rows, :]
        sig = jax.nn.sigmoid(gate)
        act = gate * sig
        h_ref[rows, :] = (act * up).astype(BF)
        gp_ref[rows, :] = (back * up * sig * (1.0 + gate * (1.0 - sig))).astype(BF)
        up_ref[rows, :] = (back * act).astype(BF)

    sort_a(0)
    multiply(0, 64, 0, WA)
    further = []
    for chunk in range(4):
        land, step, way = (1, 1, 0) if chunk < 2 else (3, 3, 1)
        forward[2 * chunk + way].wait_recv()
        rows = pl.ds(128 * chunk, 128)
        copy = remote(ra.at[land, rows, :], ra.at[2, rows, :], f2_s.at[chunk], f2_r.at[chunk], along(step))
        copy.start()
        further.append(copy)
    for chunk in range(4):
        forward[2 * chunk + (1 if chunk < 2 else 0)].wait_recv()
    sort_a(1)
    sort_a(3)
    multiply(64, 128, 0, WA)
    whole(sb, rb, early, sb_s.at[0], sb_r.at[0]).wait_recv()
    for k in (0, 1, 3):
        sort_b(k)
    multiply(0, 192, WA, WB)
    activate(0, 192)

    def parts(k, col, width, st):
        row = 64 * PLACE[k]
        rows = slice(row, row + 64)

        def one(s, _):
            cols = pl.ds(pl.multiple_of(s * WIDE + col, 128), width)
            near = dot_nt(gp_ref[rows, :], wg[cols, :]) + dot_nt(up_ref[rows, :], wu[cols, :])
            gacc[:, cols] += jnp.sum((near * xs[rows, cols].astype(F32)).reshape(8, 8, width), axis=0)
            near = near.astype(BF)
            far = dot(h_ref[rows, :], wd[:, cols]).astype(BF)
            for g in range(2):
                st[g, pl.ds(pl.multiple_of(32 * s, 32), 32), :] = near[32 * g:32 * g + 32]
                st[g, pl.ds(pl.multiple_of(128 + 32 * s, 32), 32), :] = far[32 * g:32 * g + 32]
            return 0

        lax.fori_loop(0, SEG, one, 0)

    def parts_a(k):
        parts(k, 0, WA, st_a)
        for g in range(2):
            qa[k, 256 * g:256 * g + 256, :] = dot(perm_t[...], st_a[g]).astype(BF)

    def parts_b(k):
        parts(k, WA, WB, st_b)
        at = 16 * PLACE[k]
        for g in range(2):
            qb[16 * g:16 * g + 16, at:at + 16, :] = dot(perm_t[...], st_b[g]).astype(BF).reshape(16, 16, WB)

    gacc[...] = jnp.zeros_like(gacc)
    for k in (0, 1, 3):
        parts_b(k)
    over_plane(qb, cb, early, qb_s.at[0], qb_r.at[0], True)

    sums = {}

    def send_sum(k, chunk):
        rows = pl.ds(128 * chunk, 128)
        land, step, way = (l1, 3, 0) if k == 1 else (l3, 1, 1)
        sem = 2 * chunk + way
        copy = remote(qa.at[k, rows, :], land.at[rows, :], l_s.at[sem], l_r.at[sem], along(step))
        copy.start()
        sums[k, chunk] = copy

    def add_half(k, chunk):
        rows = slice(128 * chunk, 128 * chunk + 128)
        other = half1[rows, :] if k == 1 else half3[128 * chunk - 256:128 * chunk - 128, :]
        qa[k, rows, :] = (qa[k, rows, :].astype(F32) + other.astype(F32)).astype(BF)

    parts_a(1)
    send_sum(1, 2)
    send_sum(1, 3)
    parts_a(3)
    send_sum(3, 0)
    send_sum(3, 1)

    for copy in further:
        copy.wait_recv()
    sort_a(2)
    whole(sb, rb, late, sb_s.at[1], sb_r.at[1]).wait_recv()
    sort_b(2)
    multiply(192, 64, 0, WIDE)
    activate(192, 64)
    keep = [pltpu.make_async_copy(xs, x_hbm, out_sem.at[0]), pltpu.make_async_copy(gs, g_hbm, out_sem.at[1])]
    for copy in keep:
        copy.start()
    parts_a(2)
    low, high = pl.ds(0, 256), pl.ds(256, 256)
    halves = [
        remote(qa.at[2, low, :], half1, hf_s.at[0], hf_r.at[0], along(3)),
        remote(qa.at[2, high, :], half3, hf_s.at[1], hf_r.at[1], along(1)),
    ]
    for copy in halves:
        copy.start()
    parts_b(2)
    over_plane(qb, cb, late, qb_s.at[1], qb_r.at[1], True)
    cb[0] = qb[0]
    parts_a(0)

    term = jnp.sum(gacc[...], axis=0, keepdims=True) / gain_ref[...]
    gsend[...] = jnp.zeros_like(gsend)
    for j in range(D // 128):
        at = (j // 14) * 16 + j % 14
        gsend[at:at + 1, :] = term[:, 128 * j:128 * j + 128]

    def quarter(step):
        return gsend.at[pl.ds(pl.multiple_of(lax.rem(sx + step, 4) * 16, 16), 16), :]

    gx_copies = [remote(quarter(step), gx.at[step - 1], gx_s.at[step - 1], gx_r.at[step - 1], along(step)) for step in (1, 2, 3)]
    for copy in gx_copies:
        copy.start()
    halves[0].wait_recv()
    halves[1].wait_recv()
    add_half(1, 0)
    send_sum(1, 0)
    add_half(3, 2)
    send_sum(3, 2)
    add_half(1, 1)
    send_sum(1, 1)
    add_half(3, 3)
    send_sum(3, 3)

    def send_gain(i, _):
        remote(gpart, gl.at[i], gl_s, gl_r, peer(i, False)).start()
        return 0

    for chunk in (0, 2, 1, 3):
        if chunk == 1:
            for copy in gx_copies:
                copy.wait_recv()
            gpart[...] = gsend[pl.ds(pl.multiple_of(sx * 16, 16), 16), :] + gx[0] + gx[1] + gx[2]
            for i in range(1, NE):
                send_gain(i, 0)
            gl[0] = gpart[...]
        rows = slice(128 * chunk, 128 * chunk + 128)
        sums[1, chunk].wait_recv()
        sums[3, chunk].wait_recv()
        total = qa[0, rows, :].astype(F32) + l1[rows, :].astype(F32) + l3[rows, :].astype(F32)
        qa[0, rows, :] = total.astype(BF)

        def return_a(i, _):
            at = pl.ds(16 * i, 16)
            remote(qa.at[0, at, :], ca.at[at, :], ca_s, ca_r, peer(i, True)).start()
            return 0

        for i in range(max(8 * chunk, 1), 8 * chunk + 8):
            return_a(i, 0)
    ca[0:16, :] = qa[0, 0:16, :]

    def fold(k, value):
        out = dot_tn(spread[k], value)
        return out[0:64] + out[64:128]

    whole(qb, cb, early, qb_s.at[0], qb_r.at[0]).wait_recv()
    ys_copies = {}

    def give_back(k):
        at = 16 * PLACE[k]
        ys[k] = fold(k, cb[:, at:at + 16, :].reshape(MSG, WB)).astype(BF)
        ys_copies[k] = remote(ys.at[k], xb.at[k], ys_s.at[k - 1], ys_r.at[k - 1], along(4 - k))
        ys_copies[k].start()

    give_back(1)
    give_back(3)
    mine_b = fold(0, cb[:, 0:16, :].reshape(MSG, WB))
    whole(qb, cb, late, qb_s.at[1], qb_r.at[1]).wait_recv()
    give_back(2)
    for copy in ys_copies.values():
        copy.wait_recv()
    for k in (1, 2, 3):
        mine_b = mine_b + xb[k].astype(F32)
    for s in range(SEG):
        cols = slice(s * WIDE + WA, (s + 1) * WIDE)
        ng[:, cols] = mine_b[16 * s:16 * s + 8]
        mx[:, cols] = mine_b[16 * s + 8:16 * s + 16]
    back_rows = pl.ds(16, MSG - 16)
    remote(qa.at[0, back_rows, :], ca.at[back_rows, :], ca_s, ca_r, along(1)).wait_recv()
    mine_a = fold(0, ca[...])
    for s in range(SEG):
        cols = slice(s * WIDE, s * WIDE + WA)
        ng[:, cols] = mine_a[16 * s:16 * s + 8]
        mx[:, cols] = mine_a[16 * s + 8:16 * s + 16]

    tokens = tok_ref[...].astype(F32)
    grad = ng[...]
    mixed_ref[...] = mx[...].astype(BF)
    scaled = gain_ref[...] * grad
    inner = jnp.sum(scaled * tokens, axis=1, keepdims=True)
    tg_ref[...] = (recip * scaled - tokens * (recip * recip * recip * inner / D)).astype(BF)
    remote(gl.at[pl.ds(1, 31)], gl.at[pl.ds(1, 31)], gl_s, gl_r, along(1)).wait_recv()
    gq_ref[...] = jnp.sum(gl[...], axis=0)

    for copy in tb_copies + forward + further + halves + list(sums.values()) + list(ys_copies.values()) + gx_copies:
        copy.wait_send()
    remote(sa.at[back_rows, :], sa.at[back_rows, :], sa_s, sa_r.at[0], along(1)).wait_send()
    for n, part in enumerate((early, late)):
        whole(sb, rb, part, sb_s.at[n], sb_r.at[n]).wait_send()
        whole(qb, cb, part, qb_s.at[n], qb_r.at[n]).wait_send()
    remote(qa.at[0, back_rows, :], ca.at[back_rows, :], ca_s, ca_r, along(1)).wait_send()
    remote(gl.at[pl.ds(1, 31)], gl.at[pl.ds(1, 31)], gl_s, gl_r, along(1)).wait_send()
    for copy in keep:
        copy.wait()


def weight_grads(
    x_ref, g_ref, h_ref, gp_ref, up_ref, quarter_ref, mixed_in, tg_in,
    wg_ref, wu_ref, wd_ref, mixed_ref, tg_ref, gain_ref, turned,
):
    @pl.when(pl.program_id(0) == 0)
    def _():
        turned[...] = h_ref[...].T

    turned_x = x_ref[...].T
    wg_ref[0] = dot(turned_x, gp_ref[...]).astype(BF)
    wu_ref[0] = dot(turned_x, up_ref[...]).astype(BF)
    wd_ref[0] = dot(turned[...], g_ref[...]).astype(BF)
    mixed_ref[...] = mixed_in[...]
    tg_ref[...] = tg_in[...]

    @pl.when(pl.program_id(0) == 0)
    def _():
        first = lax.axis_index("ep") * (D // 128)
        row, lane = first // 128, lax.rem(first, 128)
        two = jnp.concatenate([quarter_ref[pl.ds(row, 1), :], quarter_ref[pl.ds(row + 1, 1), :]], axis=1)
        gain_ref[...] = pltpu.roll(two, lax.rem(256 - lane, 256), 1)[0, 0:D // 128]


def on_device(tokens, out_grad, routes, gate_fixed, ramp_step, norm_gain, w_gate, w_up, w_down):
    vmem = pl.BlockSpec(memory_space=pltpu.VMEM)
    hbm = pl.BlockSpec(memory_space=pl.ANY)
    dma = pltpu.SemaphoreType.DMA
    outs = pl.pallas_call(
        layer,
        name="layer",
        out_shape=(
            jax.ShapeDtypeStruct((TOK, D), BF),
            jax.ShapeDtypeStruct((TOK, D), BF),
            jax.ShapeDtypeStruct((16, 128), F32),
            jax.ShapeDtypeStruct((256, D), BF),
            jax.ShapeDtypeStruct((256, D), BF),
            jax.ShapeDtypeStruct((256, HID), BF),
            jax.ShapeDtypeStruct((256, HID), BF),
            jax.ShapeDtypeStruct((256, HID), BF),
        ),
        in_specs=[vmem] * 6 + [hbm] * 3,
        out_specs=(vmem, vmem, vmem, hbm, hbm, vmem, vmem, vmem),
        scratch_shapes=[
            pltpu.VMEM((D, HID), BF), pltpu.VMEM((D, HID), BF), pltpu.VMEM((HID, D), BF),
            pltpu.VMEM((128, WIDE), BF),
            pltpu.VMEM((4, 64, WB + 128), BF),
            pltpu.VMEM((4, MSG, 128), BF),
            pltpu.VMEM((256, 256), BF), pltpu.VMEM((256, 256), BF),
            pltpu.VMEM((MSG, WA), BF), pltpu.VMEM((4, MSG, WA), BF),
            pltpu.VMEM((NE, 64, WB), BF), pltpu.VMEM((NE, 64, WB), BF),
            pltpu.VMEM((256, D), BF), pltpu.VMEM((256, D), BF),
            pltpu.VMEM((3, 256, HID), F32),
            pltpu.VMEM((2, 256, WA), BF), pltpu.VMEM((2, 256, WB), BF),
            pltpu.VMEM((4, MSG, WA), BF), pltpu.VMEM((NE, 64, WB), BF),
            pltpu.VMEM((256, WA), BF), pltpu.VMEM((256, WA), BF),
            pltpu.VMEM((MSG, WA), BF), pltpu.VMEM((MSG, WA), BF),
            pltpu.VMEM((MSG, WA), BF), pltpu.VMEM((NE, 64, WB), BF),
            pltpu.VMEM((4, 64, WB), BF), pltpu.VMEM((4, 64, WB), BF),
            pltpu.VMEM((TOK, D), F32), pltpu.VMEM((TOK, D), F32),
            pltpu.VMEM((8, D), F32), pltpu.VMEM((64, 128), F32), pltpu.VMEM((3, 16, 128), F32),
            pltpu.VMEM((16, 128), F32), pltpu.VMEM((NE, 16, 128), F32),
            dma((3,)), dma((2,)), dma((3,)), dma((3,)), dma, dma((4,)), dma((8,)), dma((8,)), dma((4,)), dma((4,)), dma((2,)), dma((2,)),
            dma((2,)), dma((2,)), dma((8,)), dma((8,)), dma((2,)), dma((2,)), dma, dma, dma((3,)), dma((3,)), dma((3,)), dma((3,)), dma, dma,
        ],
        compiler_params=pltpu.CompilerParams(collective_id=0, has_side_effects=True, vmem_limit_bytes=60 * 2**20),
        cost_estimate=pl.CostEstimate(flops=8 * 10**9, bytes_accessed=20 * 10**6, transcendentals=65536),
    )(tokens, out_grad, routes, gate_fixed, ramp_step.reshape(1, NE), norm_gain.reshape(1, D), w_gate[0], w_up[0], w_down[0])
    mixed, tokens_grad, quarter, rows_x, rows_g, hidden, gate_pre, up_pre = outs
    block = 3584
    tall = pl.BlockSpec((1, block, HID), lambda i: (0, i, 0))
    wide = pl.BlockSpec((256, block), lambda i: (0, i))
    few = pl.BlockSpec((TOK, block), lambda i: (0, i))
    fixed = pl.BlockSpec((256, HID), lambda i: (0, 0))
    w_gate_grad, w_up_grad, w_down_grad, mixed, tokens_grad, gain_grad = pl.pallas_call(
        weight_grads,
        name="weight_grads",
        grid=(D // block,),
        out_shape=(
            jax.ShapeDtypeStruct((1, D, HID), BF),
            jax.ShapeDtypeStruct((1, D, HID), BF),
            jax.ShapeDtypeStruct((1, HID, D), BF),
            jax.ShapeDtypeStruct((TOK, D), BF),
            jax.ShapeDtypeStruct((TOK, D), BF),
            jax.ShapeDtypeStruct((D // 128,), F32),
        ),
        in_specs=[wide, wide, fixed, fixed, fixed, pl.BlockSpec((16, 128), lambda i: (0, 0)), few, few],
        out_specs=(tall, tall, pl.BlockSpec((1, HID, block), lambda i: (0, 0, i)), few, few, pl.BlockSpec((D // 128,), lambda i: (0,))),
        scratch_shapes=[pltpu.VMEM((HID, 256), BF)],
        compiler_params=pltpu.CompilerParams(vmem_limit_bytes=60 * 2**20),
        cost_estimate=pl.CostEstimate(flops=3 * 10**9, bytes_accessed=19 * 10**6, transcendentals=0),
    )(rows_x, rows_g, hidden, gate_pre, up_pre, quarter, mixed, tokens_grad)
    return (mixed, tokens_grad, gain_grad, w_gate_grad, w_up_grad, w_down_grad)


def solution(mesh):
    return jax.shard_map(
        on_device,
        mesh=mesh,
        in_specs=(
            P(("seq", "ep"), None),
            P(("seq", "ep"), None),
            P(("seq", "ep"), None),
            P(("seq", "ep"), None),
            P(),
            P(),
            P("ep", None, "seq"),
            P("ep", None, "seq"),
            P("ep", "seq", None),
        ),
        out_specs=(
            P(("seq", "ep"), None),
            P(("seq", "ep"), None),
            P(("seq", "ep")),
            P("ep", None, "seq"),
            P("ep", None, "seq"),
            P("ep", "seq", None),
        ),
        check_vma=False,
    )
```
